256 devices in a mesh: seq: 64 (over y, x_hi, z), head: 4 (over x_lo, core).
Axes of the slice: x: 4 (x_hi: 2, x_lo: 2; x = x_hi * 2 + x_lo), y: 4, z: 8, core: 2. Of those that a mesh axis runs over, the one named last changes fastest.
Arguments:
- patches: bfloat16 [8192, 1280], P('seq'), may hold values from -6 to 6
- gain: float32 [1280], replicated, may hold values from 0.25 to 1.75
- w_qkv: bfloat16 [1280, 3, 1280], P(None, None, 'head'), may hold values from -0.15625 to 0.15625
- w_out: bfloat16 [1280, 1280], P('head'), may hold values from -0.3125 to 0.3125
- image_ids: int32 [8192], P('seq'), may hold values from 0 to 63, never falling along the last dimension, each value on 1 to 384 neighbouring positions
- cotangent: bfloat16 [8192, 1280], P('seq', 'head'), may hold values from -6 to 6
Outputs:
- attn_out: bfloat16 [8192, 1280], P('seq', 'head')
- grad_patches: bfloat16 [8192, 1280], P('seq', 'head')
- grad_w_qkv: float32 [1280, 3, 1280], P('seq', None, 'head')
- grad_w_out: float32 [1280, 1280], P('head', 'seq')
- grad_gain: float32 [1280], P('head')
The draws below stay inside these ranges and needn't reach their ends.
Inputs may be any that keep to these rules, and one draw needn't show every extreme that they name: image_ids never fall along the patches; each image holds 1 to 384 patches, and one holds exactly 384.
All inputs are finite; a program needn't handle non-finite values.
Results may differ from the reference program's by a relative error of at most 0.017.
Values may be sent and summed in bfloat16 or wider, within the bound.
No kernel may reach another device: no remote copies, remote signals or barrier semaphores. Data moves between devices by JAX's collectives and lax.ppermute only.
A program may use at most 64 MiB of HBM per device.

```python
import math
import jax
import jax.numpy as jnp
import numpy as np
from jax import lax

D = 1280
HEADS = 16
HD = 80
TOK_DEV = 128
REACH = 3
SPAN = 384
IMAGES = 64
TOKENS = 8192


def level_of(key, extent, split, least, largest):
    factor_of = 1.0
    for position, shards_of in split:
        steps = jax.random.uniform(jax.random.fold_in(jax.random.fold_in(key, 6), position), (shards_of,), jnp.float32, least / len(split), largest / len(split))
        factor_of = factor_of * jnp.repeat(jnp.exp(steps), extent[position] // shards_of).reshape((-1,) + (1,) * (len(extent) - 1 - position))
    return factor_of


def length_profile(number_of, total, most, skew):
    weights = [(1 << 20) // math.isqrt(rank ** skew) + 1 for rank in range(2, number_of + 1)]
    rest, given = total - most - (number_of - 1), [1] * (number_of - 1)
    while rest > 0:
        candidates = [i for i in range(number_of - 1) if given[i] < most]
        whole, budget = sum([weights[i] for i in candidates]), rest
        for i in candidates:
            addition = min(most - given[i], max(1, budget * weights[i] // whole), rest)
            given[i] = given[i] + addition
            rest = rest - addition
    return np.array([most] + given)


def uneven_parts(stream_key, count, total, reach, lean):
    if count == 2:
        one = jax.random.randint(stream_key, (), max(1, total - reach), min(reach, total - 1) + 1)
        return jnp.stack([one, total - one])
    lengths = jnp.asarray(length_profile(count, total, reach, lean), jnp.int32)
    pairs = (count - 1) // 2
    donor, taker = lengths[1:1 + 2 * pairs:2], lengths[2:2 + 2 * pairs:2]
    room = jnp.minimum(donor - 1, reach - taker)
    moved = jax.random.randint(jax.random.fold_in(stream_key, 1), (pairs,), 0, 1 << 20) % (room + 1)
    lengths = lengths.at[1:1 + 2 * pairs:2].set(donor - moved).at[2:2 + 2 * pairs:2].set(taker + moved)
    return lengths[jax.random.permutation(jax.random.fold_in(stream_key, 2), count)]


def bell_draw(stream_key, extent, deviation, limit, shards=(), kind=jnp.bfloat16):
    entries = deviation * jax.random.normal(stream_key, extent, jnp.float32)
    if shards:
        entries = entries * level_of(stream_key, extent, shards, -0.22, 0.18)
    return jnp.clip(entries, -limit, limit).astype(kind)


def setup_inputs(seed: int = 0) -> dict:
    seeds = jax.random.split(jax.random.key(seed), 7)
    return {
        "patches": bell_draw(seeds[0], (TOKENS, D), 1.0, 6.0, ((0, 64),)),
        "gain": jnp.clip(1.0 + 0.15 * jax.random.normal(seeds[1], (D,), jnp.float32), 0.25, 1.75),
        "w_qkv": bell_draw(seeds[2], (D, 3, D), D ** -0.5, 0.15625, ((2, 4),)),
        "w_out": bell_draw(seeds[3], (D, D), (D // 4) ** -0.5, 0.3125, ((0, 4),)),
        "image_ids": jnp.searchsorted(jnp.cumsum(uneven_parts(seeds[4], IMAGES, TOKENS, SPAN, 1)), jnp.arange(TOKENS), side="right").astype(jnp.int32),
        "cotangent": bell_draw(seeds[5], (TOKENS, D), 1.0, 6.0, ((0, 64), (1, 4))),
    }


def widen(array, fill):
    edge = jnp.full((REACH * TOK_DEV,) + array.shape[1:], fill, array.dtype)
    return jnp.concatenate([edge, array, edge], axis=0)

def window(array, block_index):
    return lax.dynamic_slice_in_dim(array, (block_index * TOK_DEV).astype(jnp.int32), (2 * REACH + 1) * TOK_DEV, 0)

def own_rows(array, block_index):
    return lax.dynamic_slice_in_dim(array, (block_index * TOK_DEV).astype(jnp.int32), TOK_DEV, 0)

def by_heads(block):
    return block.reshape(block.shape[0], HEADS, HD).astype(jnp.float32)

def rounded(block):
    return lax.optimization_barrier(block.astype(jnp.bfloat16)).astype(jnp.float32)

def masked_scores(queries, keys, query_ids, key_ids):
    raw = jnp.einsum('qhd,khd->hqk', queries, keys) * HD ** (-0.5)
    same = query_ids[:, None] == key_ids[None, :]
    return jnp.where(same[None, :, :], raw, -1e+30)

def reference(patches, gain, w_qkv, w_out, image_ids, cotangent):
    score_scale = HD ** (-0.5)
    input_f32 = patches.astype(jnp.float32)
    inv_rms = lax.rsqrt(lax.optimization_barrier(jnp.mean(input_f32 * input_f32, axis=-1)) + 1e-06)
    normed = (input_f32 * inv_rms[:, None] * gain).astype(jnp.bfloat16)
    query = jnp.dot(normed, w_qkv[:, 0, :], preferred_element_type=jnp.float32).astype(jnp.bfloat16)
    keyed = jnp.dot(normed, w_qkv[:, 1, :], preferred_element_type=jnp.float32).astype(jnp.bfloat16)
    valued = jnp.dot(normed, w_qkv[:, 2, :], preferred_element_type=jnp.float32).astype(jnp.bfloat16)
    blocks = jnp.arange(TOKENS // TOK_DEV, dtype=jnp.int32)
    key_wide = widen(keyed, 0.0)
    value_wide = widen(valued, 0.0)
    id_wide = widen(image_ids, -1)

    def forward_block(block_index):
        scores = masked_scores(by_heads(own_rows(query, block_index)), by_heads(window(key_wide, block_index)), own_rows(image_ids, block_index), window(id_wide, block_index))
        totals = jnp.log(lax.optimization_barrier(jnp.sum(jnp.exp(scores), axis=-1)))
        probs = rounded(jnp.exp(scores - totals[:, :, None]))
        ctx = jnp.einsum('hqk,khd->qhd', probs, by_heads(window(value_wide, block_index)))
        return (ctx.reshape(TOK_DEV, D).astype(jnp.bfloat16), totals.T)
    ctx_blocks, lse_blocks = lax.map(forward_block, blocks)
    context = ctx_blocks.reshape(TOKENS, D)
    lse = lse_blocks.reshape(TOKENS, HEADS)
    attn_out = jnp.dot(context, w_out, preferred_element_type=jnp.float32).astype(jnp.bfloat16)
    grad_w_out = jnp.dot(context.T, cotangent, preferred_element_type=jnp.float32)
    d_context = jnp.dot(cotangent, w_out.T, preferred_element_type=jnp.float32).astype(jnp.bfloat16)
    delta = (d_context.astype(jnp.float32) * context.astype(jnp.float32)).reshape(TOKENS, HEADS, HD).sum(-1)

    def query_block(block_index):
        keys = by_heads(window(key_wide, block_index))
        scores = masked_scores(by_heads(own_rows(query, block_index)), keys, own_rows(image_ids, block_index), window(id_wide, block_index))
        probs = jnp.exp(scores - own_rows(lse, block_index).T[:, :, None])
        d_probs = jnp.einsum('qhd,khd->hqk', by_heads(own_rows(d_context, block_index)), by_heads(window(value_wide, block_index)))
        d_scores = rounded(probs * (d_probs - own_rows(delta, block_index).T[:, :, None]))
        grad_q = jnp.einsum('hqk,khd->qhd', d_scores, keys) * score_scale
        return grad_q.reshape(TOK_DEV, D).astype(jnp.bfloat16)
    query_wide = widen(query, 0.0)
    dctx_wide = widen(d_context, 0.0)
    lse_wide = widen(lse, 0.0)
    delta_wide = widen(delta, 0.0)

    def key_block(block_index):
        queries = by_heads(window(query_wide, block_index))
        grads_out = by_heads(window(dctx_wide, block_index))
        scores = masked_scores(queries, by_heads(own_rows(keyed, block_index)), window(id_wide, block_index), own_rows(image_ids, block_index))
        probs = jnp.exp(scores - window(lse_wide, block_index).T[:, :, None])
        d_probs = jnp.einsum('qhd,khd->hqk', grads_out, by_heads(own_rows(valued, block_index)))
        d_scores = rounded(probs * (d_probs - window(delta_wide, block_index).T[:, :, None]))
        grad_k = jnp.einsum('hqk,qhd->khd', d_scores, queries) * score_scale
        grad_v = jnp.einsum('hqk,qhd->khd', rounded(probs), grads_out)
        return (grad_k.reshape(TOK_DEV, D).astype(jnp.bfloat16), grad_v.reshape(TOK_DEV, D).astype(jnp.bfloat16))
    grad_q = lax.map(query_block, blocks).reshape(TOKENS, D)
    grad_k_blocks, grad_v_blocks = lax.map(key_block, blocks)
    grad_k = grad_k_blocks.reshape(TOKENS, D)
    grad_v = grad_v_blocks.reshape(TOKENS, D)
    grads = jnp.stack([grad_q, grad_k, grad_v], axis=1)
    grad_w_qkv = jnp.einsum('tc,tje->cje', normed.astype(jnp.float32), grads.astype(jnp.float32))
    d_normed = jnp.einsum('tje,cje->tc', grads.astype(jnp.float32), w_qkv.astype(jnp.float32))
    grad_gain = lax.optimization_barrier(jnp.sum(d_normed * input_f32 * inv_rms[:, None], axis=0))
    row_total = lax.optimization_barrier(jnp.sum(gain * d_normed * input_f32, axis=-1))
    grad_patches = (inv_rms[:, None] * gain * d_normed - input_f32 * (inv_rms ** 3 * row_total / D)[:, None]).astype(jnp.bfloat16)
    return (attn_out, grad_patches, grad_w_qkv, grad_w_out, grad_gain)
```

```python
import jax
import jax.numpy as jnp
from jax import lax
from jax.experimental import pallas as pl
from jax.experimental.pallas import tpu as pltpu
from jax.sharding import Mesh, PartitionSpec as P

D = 1280
HD = 80
T = 128
HL = 4
W = HL * HD
REACH = 3
NB = 2 * REACH + 1
IDROWS = 16
SCALE = HD ** (-0.5)
LOG2E = 1.4426950408889634
SEQ = ("y", "xh", "z")
HEAD = ("xl", "c")
CH = 24
F32 = jnp.float32
BF16 = jnp.bfloat16
GROUPS = ((0, 2, 0, 5), (2, 4, 0, 7), (4, 6, 1, 7), (6, 7, 3, 7))
OWN = REACH


def attention_kernel(*refs):
    blocks = refs[:NB]
    out, kn, vn, es, ds, idk = refs[NB:]
    ids = [b[4 * W : 4 * W + 1, :].astype(F32) for b in blocks]
    for c in range(NB):
        idk[c * T : (c + 1) * T, :] = jnp.transpose(jnp.broadcast_to(ids[c], (2 * T, T)))

    def one_head(h, carry):
        def rows(b, j):
            return blocks[b][pl.ds(pl.multiple_of(j * W + h * HD, 16), HD), :]

        for c in range(NB):
            kn[c * T : (c + 1) * T, :] = jnp.transpose(rows(c, 1))
            vn[c * T : (c + 1) * T, :] = jnp.transpose(rows(c, 2))
        gq = jnp.zeros((HD, T), F32)
        ctx = jnp.zeros((HD, T), F32)
        gk = jnp.zeros((HD, T), F32)
        gv = jnp.zeros((HD, T), F32)
        for qa, qb, ka, kb in GROUPS:
            n = (qb - qa) * T
            qt = jnp.concatenate([rows(b, 0) for b in range(qa, qb)], axis=1)
            dt = jnp.concatenate([rows(b, 3) for b in range(qa, qb)], axis=1)
            idq = jnp.concatenate([ids[b] for b in range(qa, qb)], axis=1)
            esum = jnp.zeros((1, n), F32)
            dsum = jnp.zeros((1, n), F32)
            for c in range(ka, kb):
                kr = slice(c * T, (c + 1) * T)
                s = jnp.dot(kn[kr, :], qt, preferred_element_type=F32)
                dp = jnp.dot(vn[kr, :], dt, preferred_element_type=F32)
                same = idk[kr, :n] == idq
                e = jnp.exp2(jnp.where(same, s * (SCALE * LOG2E), -1e30))
                es[kr, :n] = e
                ds[kr, :n] = dp
                esum = esum + jnp.sum(e, axis=0, keepdims=True)
                dsum = dsum + jnp.sum(e * dp, axis=0, keepdims=True)
            r = 1.0 / jnp.maximum(esum, 1e-37)
            delta = dsum * r
            own = slice(OWN * T, (OWN + 1) * T)
            p = es[own, :n] * r
            dsc = (p * (ds[own, :n] - delta)).astype(BF16)
            lanes = (((1,), (1,)), ((), ()))
            gk = gk + lax.dot_general(qt, dsc, lanes, preferred_element_type=F32)
            gv = gv + lax.dot_general(dt, p.astype(BF16), lanes, preferred_element_type=F32)
            if qa <= OWN < qb:
                o = (OWN - qa) * T
                ro = r[:, o : o + T]
                do = delta[:, o : o + T]
                for c in range(ka, kb):
                    kr = slice(c * T, (c + 1) * T)
                    pc = es[kr, o : o + T] * ro
                    dc = (pc * (ds[kr, o : o + T] - do)).astype(BF16)
                    gq = gq + jnp.dot(rows(c, 1), dc, preferred_element_type=F32)
                    ctx = ctx + jnp.dot(rows(c, 2), pc.astype(BF16), preferred_element_type=F32)
        for j, val in enumerate((gq * SCALE, gk * SCALE, gv, ctx)):
            out[pl.ds(pl.multiple_of(j * W + h * HD, 16), HD), :] = val.astype(BF16)
        return carry

    lax.fori_loop(0, HL, one_head, 0)


def attention(blocks):
    return pl.pallas_call(
        attention_kernel,
        out_shape=jax.ShapeDtypeStruct((4 * W, T), BF16),
        in_specs=[pl.BlockSpec(memory_space=pltpu.VMEM)] * NB,
        out_specs=pl.BlockSpec(memory_space=pltpu.VMEM),
        scratch_shapes=[
            pltpu.VMEM((NB * T, HD), BF16),
            pltpu.VMEM((NB * T, HD), BF16),
            pltpu.VMEM((NB * T, 2 * T), F32),
            pltpu.VMEM((NB * T, 2 * T), F32),
            pltpu.VMEM((NB * T, 2 * T), F32),
        ],
        compiler_params=pltpu.CompilerParams(vmem_limit_bytes=32 * 1024 * 1024),
        name="attention",
    )(*blocks)


def weights_kernel(*refs):
    nts, cts, gts, ggs, out = refs[0:4], refs[4:8], refs[8:12], refs[12:16], refs[16]
    lanes = (((1,), (1,)), ((), ()))
    gg = ggs[0][...] + ggs[1][...] + ggs[2][...] + ggs[3][...]
    gg = jnp.concatenate([gg, jnp.zeros((1, 3 * W), F32)], axis=1)
    hi = gg.astype(BF16).astype(F32)
    lo = gg - hi

    def terms(i, carry):
        at = pl.ds(pl.multiple_of(i * 4 * CH, 4 * CH), 4 * CH)
        left = sum(
            lax.dot_general(nts[y][at, :], gts[y][: 3 * W, :], lanes, preferred_element_type=F32)
            for y in range(4)
        )
        right = sum(
            lax.dot_general(cts[y][at, :], gts[y][3 * W :, :], lanes, preferred_element_type=F32)
            for y in range(4)
        )
        term = jnp.concatenate([left, right], axis=1).reshape(4, CH, 4 * W)
        row = lax.broadcasted_iota(jnp.int32, (4, CH, 4 * W), 1)
        term = jnp.where(row == 20, hi[None], jnp.where(row == 21, lo[None], term))
        out[pl.ds(i * 4, 4)] = term.astype(BF16)
        return carry

    lax.fori_loop(0, 4, terms, 0)


def weights(nts, cts, gts, ggs):
    return pl.pallas_call(
        weights_kernel,
        out_shape=jax.ShapeDtypeStruct((16, CH, 4 * W), BF16),
        in_specs=[pl.BlockSpec(memory_space=pltpu.VMEM)] * 16,
        out_specs=pl.BlockSpec(memory_space=pltpu.VMEM),
        compiler_params=pltpu.CompilerParams(vmem_limit_bytes=32 * 1024 * 1024),
        name="weights",
    )(*nts, *cts, *gts, *ggs)


def along_seq(x, by):
    return lax.ppermute(x, SEQ, [(i, i + by) for i in range(64) if 0 <= i + by < 64])


def along_y(x, by):
    return lax.ppermute(x, "y", [(i, (i + by) % 4) for i in range(4)])


def body(patches, gain, w_qkv, w_out, image_ids, cotangent):
    here = lax.axis_index("y")
    head = lax.axis_index(HEAD)
    x = patches.astype(F32)
    inv_rms = lax.rsqrt(jnp.mean(x * x, axis=-1) + 1e-06)
    normed = (x * inv_rms[:, None] * gain).astype(BF16)
    cot = lax.all_gather(cotangent, HEAD, axis=1, tiled=True)
    proj = jnp.einsum("dje,td->jet", w_qkv, normed, preferred_element_type=F32).astype(BF16)
    d_ctx = jnp.einsum("ed,td->et", w_out, cot, preferred_element_type=F32).astype(BF16)
    ids = jnp.broadcast_to((image_ids + 1).astype(BF16)[None, :], (IDROWS, T))
    own = jnp.concatenate([proj.reshape(3 * W, T), d_ctx, ids], axis=0)
    before, after = [], []
    up = down = own
    for _ in range(REACH):
        up, down = along_seq(up, 1), along_seq(down, -1)
        before.append(up)
        after.append(down)

    def padded(rows):
        rows = jnp.transpose(rows).reshape(4, 16, D // 64, T)
        return jnp.pad(rows, ((0, 0), (0, 0), (0, CH - D // 64), (0, 0))).reshape(4, 16 * CH, T)

    pairs = jnp.concatenate([padded(normed), padded(cot)], axis=1)
    slices = [
        along_y(lax.dynamic_index_in_dim(pairs, (here + by) % 4, 0, keepdims=False), by) if by else lax.dynamic_index_in_dim(pairs, here, 0, keepdims=False)
        for by in range(4)
    ]
    grads = attention(before[::-1] + [own] + after)
    all_grads = [along_y(grads, by) if by else grads for by in range(4)]

    grads_qkv, context = grads[: 3 * W], grads[3 * W :]
    first = (((0,), (0,)), ((), ()))
    d_part = lax.dot_general(grads_qkv, w_qkv.transpose(1, 2, 0).reshape(3 * W, D), first, preferred_element_type=F32).astype(BF16)
    out_part = lax.dot_general(context, w_out, first, preferred_element_type=F32).astype(BF16)
    total = jnp.sum(grads_qkv.astype(F32) * proj.reshape(3 * W, T).astype(F32), axis=0) / inv_rms
    total_hi = total.astype(BF16)
    total_lo = (total - total_hi.astype(F32)).astype(BF16)
    totals = jnp.pad(jnp.stack([total_hi, total_lo], axis=1), ((0, 0), (0, 126)))
    pieces = jnp.concatenate(
        [
            out_part.reshape(T, 4, W).transpose(1, 0, 2),
            d_part.reshape(T, 4, W).transpose(1, 0, 2),
            jnp.broadcast_to(totals[None], (4, T, 128)),
        ],
        axis=2,
    )
    got = lax.all_to_all(pieces, HEAD, 0, 0, tiled=True)
    got = jnp.sum(got.astype(F32), axis=0)
    attn_out = got[:, :W].astype(BF16)
    d_own = got[:, W : 2 * W]
    row_total = got[:, 2 * W] + got[:, 2 * W + 1]
    x_own = lax.dynamic_slice_in_dim(x, head * W, W, 1)
    gain_own = lax.dynamic_slice_in_dim(gain, head * W, W, 0)
    grad_patches = (
        inv_rms[:, None] * gain_own * d_own - x_own * (inv_rms**3 * row_total / D)[:, None]
    ).astype(BF16)
    gg = jnp.sum(d_own * x_own * inv_rms[:, None], axis=0)[None, :]
    all_gg = [along_y(gg, by) if by else gg for by in range(4)]
    terms = weights(
        [s[: 16 * CH] for s in slices], [s[16 * CH :] for s in slices], all_grads, all_gg
    )
    terms = lax.all_to_all(terms, ("xh", "z"), 0, 0, tiled=True)
    sums = jnp.sum(terms.astype(F32), axis=0)
    grad_w_qkv = sums[:20, : 3 * W].reshape(20, 3, W)
    grad_w_out = sums[:20, 3 * W :].T
    grad_gain = sums[20, :W] + sums[21, :W]
    return (attn_out, grad_patches, grad_w_qkv, grad_w_out, grad_gain)


def solution(mesh):
    fine = Mesh(mesh.devices.reshape(4, 2, 8, 2, 2), SEQ + HEAD)
    in_specs = (
        P(SEQ, None),
        P(),
        P(None, None, HEAD),
        P(HEAD, None),
        P(SEQ),
        P(SEQ, HEAD),
    )
    out_specs = (
        P(SEQ, HEAD),
        P(SEQ, HEAD),
        P(SEQ, None, HEAD),
        P(HEAD, SEQ),
        P(HEAD),
    )
    return jax.shard_map(body, mesh=fine, in_specs=in_specs, out_specs=out_specs, check_vma=False)
```

```python
import jax
import jax.numpy as jnp
from jax import lax
from jax.experimental import pallas as pl
from jax.experimental.pallas import tpu as pltpu
from jax.sharding import Mesh, PartitionSpec as P

D = 1280
HD = 80
T = 128
HL = 4
W = HL * HD
REACH = 3
NB = 2 * REACH + 1
IDROWS = 16
SCALE = HD ** (-0.5)
LOG2E = 1.4426950408889634
SEQ = ("y", "xh", "z")
HEAD = ("xl", "c")
F32 = jnp.float32
BF16 = jnp.bfloat16
GROUPS = ((0, 2, 0, 5), (2, 4, 0, 7), (4, 6, 1, 7), (6, 7, 3, 7))
OWN = REACH


def attention_kernel(*refs):
    blocks = refs[:NB]
    out, kn, vn, es, ds, idk = refs[NB:]
    ids = [b[4 * W : 4 * W + 1, :].astype(F32) for b in blocks]
    for c in range(NB):
        idk[c * T : (c + 1) * T, :] = jnp.transpose(jnp.broadcast_to(ids[c], (2 * T, T)))

    def one_head(h, carry):
        def rows(b, j):
            return blocks[b][pl.ds(pl.multiple_of(j * W + h * HD, 16), HD), :]

        for c in range(NB):
            kn[c * T : (c + 1) * T, :] = jnp.transpose(rows(c, 1))
            vn[c * T : (c + 1) * T, :] = jnp.transpose(rows(c, 2))
        gq = jnp.zeros((HD, T), F32)
        ctx = jnp.zeros((HD, T), F32)
        gk = jnp.zeros((HD, T), F32)
        gv = jnp.zeros((HD, T), F32)
        for qa, qb, ka, kb in GROUPS:
            n = (qb - qa) * T
            qt = jnp.concatenate([rows(b, 0) for b in range(qa, qb)], axis=1)
            dt = jnp.concatenate([rows(b, 3) for b in range(qa, qb)], axis=1)
            idq = jnp.concatenate([ids[b] for b in range(qa, qb)], axis=1)
            esum = jnp.zeros((1, n), F32)
            dsum = jnp.zeros((1, n), F32)
            for c in range(ka, kb):
                kr = slice(c * T, (c + 1) * T)
                s = jnp.dot(kn[kr, :], qt, preferred_element_type=F32)
                dp = jnp.dot(vn[kr, :], dt, preferred_element_type=F32)
                same = idk[kr, :n] == idq
                e = jnp.exp2(jnp.where(same, s * (SCALE * LOG2E), -1e30))
                es[kr, :n] = e
                ds[kr, :n] = dp
                esum = esum + jnp.sum(e, axis=0, keepdims=True)
                dsum = dsum + jnp.sum(e * dp, axis=0, keepdims=True)
            r = 1.0 / jnp.maximum(esum, 1e-37)
            delta = dsum * r
            own = slice(OWN * T, (OWN + 1) * T)
            p = es[own, :n] * r
            dsc = (p * (ds[own, :n] - delta)).astype(BF16)
            lanes = (((1,), (1,)), ((), ()))
            gk = gk + lax.dot_general(qt, dsc, lanes, preferred_element_type=F32)
            gv = gv + lax.dot_general(dt, p.astype(BF16), lanes, preferred_element_type=F32)
            if qa <= OWN < qb:
                o = (OWN - qa) * T
                ro = r[:, o : o + T]
                do = delta[:, o : o + T]
                for c in range(ka, kb):
                    kr = slice(c * T, (c + 1) * T)
                    pc = es[kr, o : o + T] * ro
                    dc = (pc * (ds[kr, o : o + T] - do)).astype(BF16)
                    gq = gq + jnp.dot(rows(c, 1), dc, preferred_element_type=F32)
                    ctx = ctx + jnp.dot(rows(c, 2), pc.astype(BF16), preferred_element_type=F32)
        for j, val in enumerate((gq * SCALE, gk * SCALE, gv, ctx)):
            out[pl.ds(pl.multiple_of(j * W + h * HD, 16), HD), :] = val.astype(BF16)
        return carry

    lax.fori_loop(0, HL, one_head, 0)


def attention(blocks):
    return pl.pallas_call(
        attention_kernel,
        out_shape=jax.ShapeDtypeStruct((4 * W, T), BF16),
        in_specs=[pl.BlockSpec(memory_space=pltpu.VMEM)] * NB,
        out_specs=pl.BlockSpec(memory_space=pltpu.VMEM),
        scratch_shapes=[
            pltpu.VMEM((NB * T, HD), BF16),
            pltpu.VMEM((NB * T, HD), BF16),
            pltpu.VMEM((NB * T, 2 * T), F32),
            pltpu.VMEM((NB * T, 2 * T), F32),
            pltpu.VMEM((NB * T, 2 * T), F32),
        ],
        compiler_params=pltpu.CompilerParams(vmem_limit_bytes=32 * 1024 * 1024),
        name="attention",
    )(*blocks)


def vmem(n):
    return [pl.BlockSpec(memory_space=pltpu.VMEM)] * n


def call(kernel, name, outs, scratch, scalars, *args):
    single = not isinstance(outs, (list, tuple))
    result = pl.pallas_call(
        kernel,
        out_shape=outs,
        in_specs=[pl.BlockSpec(memory_space=pltpu.SMEM)] * len(scalars) + vmem(len(args)),
        out_specs=pl.BlockSpec(memory_space=pltpu.VMEM) if single else vmem(len(outs)),
        scratch_shapes=scratch,
        compiler_params=pltpu.CompilerParams(vmem_limit_bytes=32 * 1024 * 1024),
        name=name,
    )(*scalars, *args)
    return result


def shape(dims, dtype=BF16):
    return jax.ShapeDtypeStruct(dims, dtype)


def project_kernel(head, patches, gain, w, proj, normed, x_own, scale_own, inv_out, xt):
    xt[...] = jnp.transpose(patches[...])
    x = xt[...].astype(F32)
    inv = lax.rsqrt(jnp.sum(x * x, axis=0, keepdims=True) * (1.0 / D) + 1e-06)
    g = jnp.transpose(jnp.broadcast_to(gain[...], (T, D)))
    scale = inv * g
    normed[...] = (x * inv * g).astype(BF16)
    proj[...] = jnp.dot(w[...], normed[...], preferred_element_type=F32).astype(BF16)
    inv_out[...] = jnp.broadcast_to(inv, (8, T))
    for j in range(4):
        @pl.when(head[0] == j)
        def _():
            x_own[...] = xt[j * W : (j + 1) * W, :]
            scale_own[...] = scale[j * W : (j + 1) * W, :]


def payload_kernel(head, here, c0, c1, c2, c3, w_out, proj, normed, ids, own, s0, s1, s2, s3, cot):
    for k, piece in enumerate((c0, c1, c2, c3)):
        cot[pl.ds(pl.multiple_of(jnp.bitwise_xor(head[0], k) * W, W), W), :] = piece[...]
    own[: 3 * W, :] = proj[...]
    own[3 * W : 4 * W, :] = jnp.dot(w_out[...], cot[...], preferred_element_type=F32).astype(BF16)
    own[4 * W :, :] = jnp.broadcast_to((ids[...] + 1).astype(F32), (IDROWS, T)).astype(BF16)
    for by, out in enumerate((s0, s1, s2, s3)):
        at = pl.ds(pl.multiple_of(lax.rem(here[0] + by, 4) * W, W), W)
        out[:W, :] = normed[at, :]
        out[W:, :] = cot[at, :]


def pieces_kernel(grads, own, w, w_out, out):
    total = jnp.sum(grads[: 3 * W, :].astype(F32) * own[: 3 * W, :].astype(F32), axis=0, keepdims=True)
    hi = total.astype(BF16).astype(F32)
    row = lax.broadcasted_iota(jnp.int32, (IDROWS, T), 0)
    tail = jnp.where(row == 0, hi, jnp.where(row == 1, total - hi, 0.0)).astype(BF16)
    g = jnp.transpose(grads[...])
    d_part = jnp.dot(g[:, : 3 * W], w[...], preferred_element_type=F32)
    out_part = jnp.dot(g[:, 3 * W :], w_out[...], preferred_element_type=F32)
    d_part = jnp.transpose(d_part.astype(BF16))
    out_part = jnp.transpose(out_part.astype(BF16))
    for j in range(4):
        out[j, :W, :] = out_part[j * W : (j + 1) * W, :]
        out[j, W : 2 * W, :] = d_part[j * W : (j + 1) * W, :]
        out[j, 2 * W :, :] = tail


def rows_kernel(got, x_own, scale_own, inv, attn_out, grad_patches, gg):
    total = got[0].astype(F32) + got[1].astype(F32) + got[2].astype(F32) + got[3].astype(F32)
    attn_out[...] = total[:W, :].astype(BF16)
    d_own = total[W : 2 * W, :]
    x = x_own[...].astype(F32)
    i = inv[0:1, :]
    row_total = total[2 * W : 2 * W + 1, :] + total[2 * W + 1 : 2 * W + 2, :]
    grad_patches[...] = (scale_own[...] * d_own - x * (i * i * row_total * (1.0 / D))).astype(BF16)
    part = jnp.transpose(d_own * x * i)
    part = jnp.sum(part, axis=0, keepdims=True)
    part = jnp.concatenate([part, jnp.zeros((1, 64), F32)], axis=1)
    row = lax.broadcasted_iota(jnp.int32, (8, T), 0)
    gg[...] = jnp.where(
        row == 0, part[:, :T], jnp.where(row == 1, part[:, T : 2 * T], jnp.where(row == 2, part[:, 2 * T :], 0.0))
    )


def weights_kernel(*refs):
    ss, gs, ggs, out, term = refs[0:4], refs[4:8], refs[8:12], refs[12], refs[13]
    lanes = (((1,), (1,)), ((), ()))
    gg = ggs[0][...] + ggs[1][...] + ggs[2][...] + ggs[3][...]
    hi = gg.astype(BF16).astype(F32)
    tail = hi + pltpu.roll(gg - hi, 4, 0)
    n = jnp.concatenate([s[:W, :] for s in ss], axis=1)
    c = jnp.concatenate([s[W:, :] for s in ss], axis=1)
    g = jnp.concatenate([r[: 3 * W, :] for r in gs], axis=1)
    x = jnp.concatenate([r[3 * W :, :] for r in gs], axis=1)
    term[:, : 3 * W] = lax.dot_general(n, g, lanes, preferred_element_type=F32)
    term[:, 3 * W :] = lax.dot_general(c, x, lanes, preferred_element_type=F32)
    for i in range(16):
        rows = [term[20 * i : 20 * i + 20, T * l : T * (l + 1)] for l in range(10)]
        out[i] = jnp.concatenate(rows + [tail], axis=0).astype(BF16)


def sums_kernel(got, qkv, out, gg):
    total = got[0].astype(F32)
    for i in range(1, 16):
        total = total + got[i].astype(F32)
    full = jnp.concatenate([total[20 * l : 20 * l + 20, :] for l in range(10)], axis=1)
    for j in range(3):
        qkv[j] = full[:, j * W : (j + 1) * W]
    out[...] = full[:, 3 * W :]
    tail = total[200:208, :]
    tail = tail + pltpu.roll(tail, 4, 0)
    gg[...] = jnp.concatenate([tail[0:1, :], tail[1:2, :], tail[2:3, :64]], axis=1)


def along_seq(x, by):
    return lax.ppermute(x, SEQ, [(i, i + by) for i in range(64) if 0 <= i + by < 64])


def along_y(x, by):
    return lax.ppermute(x, "y", [(i, (i + by) % 4) for i in range(4)])


def along_head(x, by):
    return lax.ppermute(x, HEAD, [(i, i ^ by) for i in range(4)])


def body(patches, gain, w_qkv, w_out, image_ids, cotangent):
    here = lax.axis_index("y").astype(jnp.int32).reshape(1)
    head = lax.axis_index(HEAD).astype(jnp.int32).reshape(1)
    cot = cotangent.T
    cots = [along_head(cot, k) if k else cot for k in range(4)]
    w = w_qkv.transpose(1, 2, 0).reshape(3 * W, D)
    proj, normed, x_own, scale_own, inv = call(
        project_kernel,
        "project",
        [shape((3 * W, T)), shape((D, T)), shape((W, T)), shape((W, T), F32), shape((8, T), F32)],
        [pltpu.VMEM((D, T), BF16)],
        [head],
        patches,
        gain.reshape(1, D),
        w,
    )
    own, *slices = call(
        payload_kernel,
        "payload",
        [shape((4 * W + IDROWS, T))] + [shape((2 * W, T))] * 4,
        [pltpu.VMEM((D, T), BF16)],
        [head, here],
        *cots,
        w_out,
        proj,
        normed,
        image_ids.reshape(1, T),
    )
    before, after = [], []
    up = down = own
    for _ in range(REACH):
        up, down = along_seq(up, 1), along_seq(down, -1)
        before.append(up)
        after.append(down)
    slices = [along_y(s, by) if by else s for by, s in enumerate(slices)]
    grads = attention(before[::-1] + [own] + after)
    all_grads = [along_y(grads, by) if by else grads for by in range(4)]
    pieces = call(pieces_kernel, "pieces", shape((4, 2 * W + IDROWS, T)), [], [], grads, own, w, w_out)
    got = lax.all_to_all(pieces, HEAD, 0, 0, tiled=True)
    attn_out, grad_patches, gg = call(
        rows_kernel,
        "rows",
        [shape((W, T)), shape((W, T)), shape((8, T), F32)],
        [],
        [],
        got,
        x_own,
        scale_own,
        inv,
    )
    all_gg = [along_y(gg, by) if by else gg for by in range(4)]
    terms = call(
        weights_kernel,
        "weights",
        shape((16, 208, T)),
        [pltpu.VMEM((W, 4 * W), F32)],
        [],
        *slices,
        *all_grads,
        *all_gg,
    )
    terms = lax.all_to_all(terms, ("xh", "z"), 0, 0, tiled=True)
    grad_w_qkv, grad_w_out, grad_gain = call(
        sums_kernel,
        "sums",
        [shape((3, 20, W), F32), shape((20, W), F32), shape((1, W), F32)],
        [],
        [],
        terms,
    )
    return (attn_out.T, grad_patches.T, grad_w_qkv.transpose(1, 0, 2), grad_w_out.T, grad_gain.reshape(W))


def solution(mesh):
    fine = Mesh(mesh.devices.reshape(4, 2, 8, 2, 2), SEQ + HEAD)
    in_specs = (
        P(SEQ, None),
        P(),
        P(None, None, HEAD),
        P(HEAD, None),
        P(SEQ),
        P(SEQ, HEAD),
    )
    out_specs = (
        P(SEQ, HEAD),
        P(SEQ, HEAD),
        P(SEQ, None, HEAD),
        P(HEAD, SEQ),
        P(HEAD),
    )
    return jax.shard_map(body, mesh=fine, in_specs=in_specs, out_specs=out_specs, check_vma=False)
```

```python
import jax
import jax.numpy as jnp
from jax import lax
from jax.experimental import pallas as pl
from jax.experimental.pallas import tpu as pltpu
from jax.sharding import Mesh, PartitionSpec as P

D = 1280
HD = 80
T = 128
HL = 4
W = HL * HD
IDROWS = 16
R = 4 * HD + IDROWS
WIN = 10
OWN = 3
SCALE = HD ** (-0.5)
LOG2E = 1.4426950408889634
SEQ = ("y", "xh", "z")
HEAD = ("xl", "c")
F32 = jnp.float32
BF16 = jnp.bfloat16
LANES = (((1,), (1,)), ((), ()))
GROUPS = ((0, 2, 0, 5), (2, 4, 0, 7), (4, 6, 1, 9), (6, 8, 3, 10), (8, 10, 5, 10))


def call(kernel, name, outs, scratch, scalars, *args, far=0, far_outs=0, limit=12):
    single = not isinstance(outs, (list, tuple))
    vmem, hbm = pl.BlockSpec(memory_space=pltpu.VMEM), pl.BlockSpec(memory_space=pltpu.HBM)
    specs = [pl.BlockSpec(memory_space=pltpu.SMEM)] * len(scalars)
    specs += [vmem] * (len(args) - far) + [hbm] * far
    return pl.pallas_call(
        kernel,
        out_shape=outs,
        in_specs=specs,
        out_specs=vmem if single else [vmem] * (len(outs) - far_outs) + [hbm] * far_outs,
        scratch_shapes=scratch,
        compiler_params=pltpu.CompilerParams(vmem_limit_bytes=limit * 1024 * 1024),
        cost_estimate=pl.CostEstimate(flops=1000, bytes_accessed=1000, transcendentals=0),
        name=name,
    )(*scalars, *args)


def fetch(sems, *pairs):
    copies = [pltpu.make_async_copy(src, dst, sems.at[i]) for i, (src, dst) in enumerate(pairs)]
    for copy in copies:
        copy.start()
    return copies


def shape(dims, dtype=BF16):
    return jax.ShapeDtypeStruct(dims, dtype)


def times(index, size):
    return pl.ds(pl.multiple_of(index * size, size), size)


def norm_kernel(head, patches_far, gain_far, cot_far, normed, quarter, x_own, scale_own, inv_out, patches, gain, xt, scale, sems):
    copies = fetch(sems, (patches_far, patches), (gain_far, gain), (cot_far, quarter.at[W:]))
    copies[0].wait()
    copies[1].wait()
    xt[...] = jnp.transpose(patches[...])
    x = xt[...].astype(F32)
    inv = lax.rsqrt(jnp.sum(x * x, axis=0, keepdims=True) * (1.0 / D) + 1e-06)
    for l in range(10):
        rows = slice(l * T, (l + 1) * T)
        g = jnp.transpose(jnp.broadcast_to(gain[l : l + 1, :], (T, T)))
        scale[rows, :] = inv * g
        normed[rows, :] = (xt[rows, :].astype(F32) * inv * g).astype(BF16)
    inv_out[...] = jnp.broadcast_to(inv, (8, T))
    at = times(head[0], W)
    x_own[...] = xt[at, :]
    scale_own[...] = scale[at, :]
    quarter[:W, :] = normed[at, :]
    copies[2].wait()


def project_kernel(normed, w, w_out, ids, proj):
    proj[...] = jnp.dot(w[...], normed[...], preferred_element_type=F32).astype(BF16)


def payload_kernel(head, c0, c1, c2, c3, proj, w_out, ids, own, cot):
    for k, piece in enumerate((c0, c1, c2, c3)):
        cot[times(jnp.bitwise_xor(head[0], k), W), :] = piece[...]
    d_ctx = jnp.dot(w_out[...], cot[...], preferred_element_type=F32).astype(BF16)
    id_rows = jnp.broadcast_to((ids[...] + 1).astype(F32), (IDROWS, T)).astype(BF16)
    for m in range(HL):
        rows = [proj[j * W + m * HD : j * W + (m + 1) * HD, :] for j in range(3)]
        rows = rows + [d_ctx[m * HD : (m + 1) * HD, :], id_rows]
        for u in range(2):
            for j, block in enumerate(rows):
                own[4 * u + m, j * HD : j * HD + block.shape[0], :] = block


def attention_kernel(zz, local, halo, grads, o0, o1, o2, o3, win, kn, vn, idk, es, ds, ps, dss, gk, gv, sems):
    u, m = lax.div(zz[0], 4), lax.rem(zz[0], 4)

    @pl.when(u == 0)
    def _():
        win[:3] = halo[...]
        win[3:] = local[:7]

    @pl.when(u == 1)
    def _():
        win[:7] = local[1:]
        win[7:] = halo[...]

    def rows(c, j):
        return win[c, j * HD : (j + 1) * HD, :]

    def side(first, last, j):
        return jnp.concatenate([rows(c, j) for c in range(first, last)], axis=1)

    ids = [win[c, 4 * HD : 4 * HD + 1, :].astype(F32) for c in range(WIN)]
    for c in range(WIN):
        at = slice(c * T, (c + 1) * T)
        idk[at, :] = jnp.transpose(jnp.broadcast_to(ids[c], (2 * T, T)))
        kn[at, :] = jnp.transpose(rows(c, 1))
        vn[at, :] = jnp.transpose(rows(c, 2))
    gk[...] = jnp.zeros(gk.shape, F32)
    gv[...] = jnp.zeros(gv.shape, F32)
    for qa, qb, ka, kb in GROUPS:
        n = (qb - qa) * T
        qt, dt = side(qa, qb, 0), side(qa, qb, 3)
        idq = jnp.concatenate(ids[qa:qb], axis=1)
        esum = jnp.zeros((1, n), F32)
        dsum = jnp.zeros((1, n), F32)
        for c in range(ka, kb):
            kr = slice(c * T, (c + 1) * T)
            s = jnp.dot(kn[kr, :], qt, preferred_element_type=F32)
            dp = jnp.dot(vn[kr, :], dt, preferred_element_type=F32)
            e = jnp.exp2(jnp.where(idk[kr, :] == idq, s * (SCALE * LOG2E), -1e30))
            es[kr, :] = e
            ds[kr, :] = dp
            esum = esum + jnp.sum(e, axis=0, keepdims=True)
            dsum = dsum + jnp.sum(e * dp, axis=0, keepdims=True)
        r = 1.0 / jnp.maximum(esum, 1e-37)
        delta = dsum * r
        qs, qe = max(qa, OWN), min(qb, OWN + 4)
        ks, ke = max(ka, OWN), min(kb, OWN + 4)
        for c in range(ka, kb) if qs < qe else range(ks, ke):
            kr = slice(c * T, (c + 1) * T)
            p = es[kr, :] * r
            ps[kr, :] = p.astype(BF16)
            dss[kr, :] = (p * (ds[kr, :] - delta)).astype(BF16)
        own = slice(ks * T, ke * T)
        to = slice((ks - OWN) * T, (ke - OWN) * T)
        gk[:, to] += lax.dot_general(qt, dss[own, :], LANES, preferred_element_type=F32)
        gv[:, to] += lax.dot_general(dt, ps[own, :], LANES, preferred_element_type=F32)
        if qs < qe:
            cols = slice((qs - qa) * T, (qe - qa) * T)
            kr = slice(ka * T, kb * T)
            gq = jnp.dot(side(ka, kb, 1), dss[kr, cols], preferred_element_type=F32) * SCALE
            ctx = jnp.dot(side(ka, kb, 2), ps[kr, cols], preferred_element_type=F32)
            for i in range(qe - qs):
                lane = slice(i * T, (i + 1) * T)
                grads[qs - OWN + i, :HD, :] = gq[:, lane].astype(BF16)
                grads[qs - OWN + i, 3 * HD :, :] = ctx[:, lane].astype(BF16)
    for i in range(4):
        lane = slice(i * T, (i + 1) * T)
        grads[i, HD : 2 * HD, :] = (gk[:, lane] * SCALE).astype(BF16)
        grads[i, 2 * HD : 3 * HD, :] = gv[:, lane].astype(BF16)
    o0[...] = grads[m]
    outs = enumerate((o1, o2, o3), 1)
    for copy in fetch(sems, *[(grads.at[jnp.bitwise_xor(m, k)], out) for k, out in outs]):
        copy.wait()


def attention(zz, local, halo):
    big = (WIN * T, 2 * T)
    return call(
        attention_kernel,
        "attention",
        [shape((4, 4 * HD, T))] + [shape((4 * HD, T))] * 4,
        [
            pltpu.VMEM((WIN, R, T), BF16),
            pltpu.VMEM((WIN * T, HD), BF16),
            pltpu.VMEM((WIN * T, HD), BF16),
            pltpu.VMEM(big, F32),
            pltpu.VMEM(big, F32),
            pltpu.VMEM(big, F32),
            pltpu.VMEM(big, BF16),
            pltpu.VMEM(big, BF16),
            pltpu.VMEM((HD, 4 * T), F32),
            pltpu.VMEM((HD, 4 * T), F32),
            pltpu.SemaphoreType.DMA((3,)),
        ],
        [zz],
        local,
        halo,
        far_outs=3,
    )


def pieces_kernel(zz, head, b0, b1, b2, b3, proj, w, w_out, p0, p1, p2, p3, grads, parts, sems):
    m = lax.rem(zz[0], 4)
    for k, piece in enumerate((b0, b1, b2, b3)):
        other = jnp.bitwise_xor(m, k)
        for j in range(4):
            grads[times(j * HL + other, HD), :] = piece[j * HD : (j + 1) * HD, :]
    total = jnp.sum(grads[: 3 * W, :].astype(F32) * proj[...].astype(F32), axis=0, keepdims=True)
    hi = total.astype(BF16).astype(F32)
    row = lax.broadcasted_iota(jnp.int32, (IDROWS, T), 0)
    tail = jnp.where(row == 0, hi, jnp.where(row == 1, total - hi, 0.0)).astype(BF16)
    g = jnp.transpose(grads[...])
    d_part = jnp.dot(g[:, : 3 * W], w[...], preferred_element_type=F32)
    out_part = jnp.dot(g[:, 3 * W :], w_out[...], preferred_element_type=F32)
    out_part = jnp.transpose(out_part.astype(BF16))
    d_part = jnp.transpose(d_part.astype(BF16))
    for j in range(4):
        parts[j, :W, :] = out_part[j * W : (j + 1) * W, :]
        parts[j, W : 2 * W, :] = d_part[j * W : (j + 1) * W, :]
        parts[j, 2 * W :, :] = tail
    p0[...] = parts[head[0]]
    outs = enumerate((p1, p2, p3), 1)
    for copy in fetch(sems, *[(parts.at[jnp.bitwise_xor(head[0], k)], out) for k, out in outs]):
        copy.wait()


def rows_kernel(g0, g1, g2, g3, x_own, scale_own, inv, attn_out, grad_patches):
    total = g0[...].astype(F32) + g1[...].astype(F32) + g2[...].astype(F32) + g3[...].astype(F32)
    attn_out[...] = total[:W, :].astype(BF16)
    d_own = total[W : 2 * W, :]
    x = x_own[...].astype(F32)
    i = inv[0:1, :]
    row_total = total[2 * W : 2 * W + 1, :] + total[2 * W + 1 : 2 * W + 2, :]
    grad_patches[...] = (scale_own[...] * d_own - x * (i * i * row_total * (1.0 / D))).astype(BF16)


def assemble_kernel(head, h0, h1, h2, h3, n, c):
    for j, quarter in enumerate((h0, h1, h2, h3)):
        at = times(jnp.bitwise_xor(head[0], j), W)
        for k in range(4):
            lane = slice(k * T, (k + 1) * T)
            n[at, lane] = quarter[2 * k * W : (2 * k + 1) * W, :]
            c[at, lane] = quarter[(2 * k + 1) * W : (2 * k + 2) * W, :]


def weights_kernel(zz, n, c, grads, gain, w, out, g, term):
    m = lax.rem(zz[0], 4)
    for k in range(4):
        g[:, k * T : (k + 1) * T] = grads[jnp.bitwise_xor(m, k)]
    left = lax.dot_general(n[...], g[: 3 * HD, :], LANES, preferred_element_type=F32)
    right = lax.dot_general(c[...], g[3 * HD :, :], LANES, preferred_element_type=F32)
    term[...] = jnp.concatenate([left, right], axis=1)
    turned = lax.dot_general(g[: 3 * HD, :], n[...], LANES, preferred_element_type=F32)
    gg = jnp.zeros((1, D), F32)
    for j in range(3):
        product = turned[j * HD : (j + 1) * HD, :] * w[times(j * HL + m, HD), :].astype(F32)
        gg = gg + jnp.sum(product, axis=0, keepdims=True)
    rows = [gg[:, l * T : (l + 1) * T] / gain[l : l + 1, :] for l in range(10)]
    rows = rows + [jnp.zeros((6, T), F32)]
    tail = jnp.concatenate(rows, axis=0).astype(BF16)
    for d in range(8):
        out[d, :160, :] = term[160 * d : 160 * d + 160, :T].astype(BF16)
        out[d, 160:320, :] = term[160 * d : 160 * d + 160, T : 2 * T].astype(BF16)
        halves = [term[160 * d + 80 * i : 160 * d + 80 * i + 80, 2 * T :] for i in range(2)]
        out[d, 320:400, :] = jnp.concatenate(halves, axis=1).astype(BF16)
        out[d, 400:, :] = tail


def middle_kernel(got, out, total):
    total[...] = sum(got[i].astype(F32) for i in range(8))
    zero = jnp.zeros((4, T), F32)
    for z in range(8):
        third = total[320 + 20 * (z % 4) : 340 + 20 * (z % 4), :]
        if z >= 4:
            third = pltpu.roll(third, 64, 1)
        rows = [total[20 * z : 20 * z + 20, :], total[160 + 20 * z : 180 + 20 * z, :], third]
        out[z] = jnp.concatenate(rows + [zero, total[400:, :]], axis=0).astype(BF16)


def sums_kernel(got, qkv, out, gg):
    tail = jnp.zeros((16, T), F32)
    cols = []
    for m in range(HL):
        total = got[m].astype(F32) + got[4 + m].astype(F32)
        cols.append(jnp.concatenate([total[20 * l : 20 * l + 20, :] for l in range(3)], axis=1))
        tail = tail + total[64:80, :]
    for j in range(3):
        qkv[j] = jnp.concatenate([x[:, j * HD : (j + 1) * HD] for x in cols], axis=1)
    out[...] = jnp.concatenate([x[:, 3 * HD : 4 * HD] for x in cols], axis=1)
    gg[...] = tail


def gain_kernel(head, t0, t1, t2, t3, out):
    total = t0[...] + t1[...] + t2[...] + t3[...]
    flat = jnp.concatenate([total[l : l + 1, :] for l in range(10)], axis=1)
    for j in range(4):
        @pl.when(head[0] == j)
        def _():
            out[...] = flat[:, j * W : (j + 1) * W]


def along_z(x, by):
    return lax.ppermute(x, "z", [(i, i ^ by) for i in range(8)]) if by else x


def along_head(x, by):
    return lax.ppermute(x, HEAD, [(i, i ^ by) for i in range(4)]) if by else x


def to_next_group(x):
    pairs = []
    for i in range(64):
        group = i // 8 + (1 if i % 8 < 4 else -1)
        if 0 <= group < 8:
            pairs.append((i, group * 8 + i % 8))
    return lax.ppermute(x, SEQ, pairs)


def body(patches, gain, w_qkv, w_out, image_ids, cotangent):
    head = lax.axis_index(HEAD).astype(jnp.int32).reshape(1)
    zz = lax.axis_index("z").astype(jnp.int32).reshape(1)
    cot = cotangent.T
    gain = gain.reshape(10, T)
    w = w_qkv.transpose(1, 2, 0).reshape(3 * W, D)
    normed, quarter, x_own, scale_own, inv = call(
        norm_kernel,
        "norm",
        [shape((D, T)), shape((2 * W, T)), shape((W, T)), shape((W, T), F32), shape((8, T), F32)],
        [
            pltpu.VMEM((T, D), BF16),
            pltpu.VMEM((10, T), F32),
            pltpu.VMEM((D, T), BF16),
            pltpu.VMEM((D, T), F32),
            pltpu.SemaphoreType.DMA((3,)),
        ],
        [head],
        patches,
        gain,
        cot,
        far=3,
        limit=60,
    )
    cot, normed = lax.optimization_barrier((cot, normed))
    cots = [along_head(cot, k) for k in range(4)]
    quarter = jnp.concatenate([along_z(quarter, k) for k in range(4)], axis=0)
    ids = image_ids.reshape(1, T)
    proj = call(project_kernel, "project", shape((3 * W, T)), [], [], normed, w, w_out, ids)
    own = call(
        payload_kernel,
        "payload",
        shape((8, R, T)),
        [pltpu.VMEM((D, T), BF16)],
        [head],
        *cots,
        proj,
        w_out,
        ids,
    )
    own, quarter = lax.optimization_barrier((own, quarter))
    local = lax.all_to_all(own, "z", 0, 0, tiled=True)
    near = lax.dynamic_slice_in_dim(local, jnp.where(zz[0] < 4, 5, 0), 3, 0)
    across = along_head(quarter, 2)
    near, across = lax.optimization_barrier((near, across))
    halo = to_next_group(near)
    quarters = [quarter, along_head(quarter, 1), across, along_head(across, 1)]
    n, c = call(
        assemble_kernel, "assemble", [shape((D, 4 * T))] * 2, [], [head], *quarters
    )
    halo, n, c = lax.optimization_barrier((halo, n, c))
    grads, *backs = attention(zz, local, halo)
    terms = call(
        weights_kernel,
        "weights",
        shape((8, 416, T)),
        [pltpu.VMEM((W, 4 * T), BF16), pltpu.VMEM((D, W), F32)],
        [zz],
        n,
        c,
        grads,
        gain,
        w,
    )
    backs, terms = lax.optimization_barrier((backs, terms))
    terms = lax.all_to_all(terms, ("y", "xh"), 0, 0, tiled=True)
    backs = [along_z(b, k) for k, b in enumerate(backs)]
    pieces = call(
        pieces_kernel,
        "pieces",
        [shape((2 * W + IDROWS, T))] * 4,
        [
            pltpu.VMEM((4 * W, T), BF16),
            pltpu.VMEM((4, 2 * W + IDROWS, T), BF16),
            pltpu.SemaphoreType.DMA((3,)),
        ],
        [zz, head],
        *backs,
        proj,
        w,
        w_out,
        far_outs=3,
    )
    terms, pieces = lax.optimization_barrier((terms, pieces))
    got = [along_head(p, k) for k, p in enumerate(pieces)]
    terms = call(middle_kernel, "middle", shape((8, 80, T)), [pltpu.VMEM((416, T), F32)], [], terms)
    terms = lax.all_to_all(terms, "z", 0, 0, tiled=True)
    terms, got = lax.optimization_barrier((terms, got))
    attn_out, grad_patches = call(
        rows_kernel,
        "rows",
        [shape((W, T)), shape((W, T))],
        [],
        [],
        *got,
        x_own,
        scale_own,
        inv,
    )
    grad_w_qkv, grad_w_out, gg = call(
        sums_kernel,
        "sums",
        [shape((3, 20, W), F32), shape((20, W), F32), shape((16, T), F32)],
        [],
        [],
        terms,
    )
    grad_gain = call(
        gain_kernel, "gain", shape((1, W), F32), [], [head], *[along_head(gg, k) for k in range(4)]
    )
    return (attn_out.T, grad_patches.T, grad_w_qkv.transpose(1, 0, 2), grad_w_out.T, grad_gain.reshape(W))


def solution(mesh):
    fine = Mesh(mesh.devices.reshape(4, 2, 8, 2, 2), SEQ + HEAD)
    in_specs = (
        P(SEQ, None),
        P(),
        P(None, None, HEAD),
        P(HEAD, None),
        P(SEQ),
        P(SEQ, HEAD),
    )
    out_specs = (
        P(SEQ, HEAD),
        P(SEQ, HEAD),
        P(SEQ, None, HEAD),
        P(HEAD, SEQ),
        P(HEAD),
    )
    return jax.shard_map(body, mesh=fine, in_specs=in_specs, out_specs=out_specs, check_vma=False)
```

```python
import jax
import jax.numpy as jnp
from jax import lax
from jax.experimental import pallas as pl
from jax.experimental.pallas import tpu as pltpu
from jax.sharding import Mesh, PartitionSpec as P

D = 1280
HD = 80
T = 128
HL = 4
W = HL * HD
IDROWS = 16
R = 4 * HD + IDROWS
WIN = 10
OWN = 3
SCALE = HD ** (-0.5)
LOG2E = 1.4426950408889634
SEQ = ("y", "xh", "z")
HEAD = ("xl", "c")
F32 = jnp.float32
BF16 = jnp.bfloat16
LANES = (((1,), (1,)), ((), ()))
GROUPS = ((0, 2, 0, 5), (2, 4, 0, 7), (4, 6, 1, 9), (6, 8, 3, 10), (8, 10, 5, 10))


def call(kernel, name, outs, scratch, scalars, *args, far=0, far_outs=0, limit=12):
    single = not isinstance(outs, (list, tuple))
    vmem, hbm = pl.BlockSpec(memory_space=pltpu.VMEM), pl.BlockSpec(memory_space=pltpu.HBM)
    specs = [pl.BlockSpec(memory_space=pltpu.SMEM)] * len(scalars)
    specs += [vmem] * (len(args) - far) + [hbm] * far
    return pl.pallas_call(
        kernel,
        out_shape=outs,
        in_specs=specs,
        out_specs=vmem if single else [vmem] * (len(outs) - far_outs) + [hbm] * far_outs,
        scratch_shapes=scratch,
        compiler_params=pltpu.CompilerParams(vmem_limit_bytes=limit * 1024 * 1024),
        cost_estimate=pl.CostEstimate(flops=1000, bytes_accessed=1000, transcendentals=0),
        name=name,
    )(*scalars, *args)


def fetch(sems, *pairs):
    copies = [pltpu.make_async_copy(src, dst, sems.at[i]) for i, (src, dst) in enumerate(pairs)]
    for copy in copies:
        copy.start()
    return copies


def shape(dims, dtype=BF16):
    return jax.ShapeDtypeStruct(dims, dtype)


def times(index, size):
    return pl.ds(pl.multiple_of(index * size, size), size)


def norm_kernel(head, patches_far, gain_far, cot_far, normed, quarter, x_own, scale_own, inv_out, patches, gain, xt, scale, sems):
    copies = fetch(sems, (patches_far, patches), (gain_far, gain), (cot_far, quarter.at[W:]))
    copies[0].wait()
    copies[1].wait()
    xt[...] = jnp.transpose(patches[...])
    x = xt[...].astype(F32)
    inv = lax.rsqrt(jnp.sum(x * x, axis=0, keepdims=True) * (1.0 / D) + 1e-06)
    for l in range(10):
        rows = slice(l * T, (l + 1) * T)
        g = jnp.transpose(jnp.broadcast_to(gain[l : l + 1, :], (T, T)))
        scale[rows, :] = inv * g
        normed[rows, :] = (xt[rows, :].astype(F32) * inv * g).astype(BF16)
    inv_out[...] = jnp.broadcast_to(inv, (8, T))
    at = times(head[0], W)
    x_own[...] = xt[at, :]
    scale_own[...] = scale[at, :]
    quarter[:W, :] = normed[at, :]
    copies[2].wait()


def project_kernel(normed, w, w_out, ids, proj):
    proj[...] = jnp.dot(w[...], normed[...], preferred_element_type=F32).astype(BF16)


def payload_kernel(head, c0, c1, c2, c3, proj, w_out, ids, own, cot):
    for k, piece in enumerate((c0, c1, c2, c3)):
        cot[times(jnp.bitwise_xor(head[0], k), W), :] = piece[...]
    d_ctx = jnp.dot(w_out[...], cot[...], preferred_element_type=F32).astype(BF16)
    id_rows = jnp.broadcast_to((ids[...] + 1).astype(F32), (IDROWS, T)).astype(BF16)
    for m in range(HL):
        rows = [proj[j * W + m * HD : j * W + (m + 1) * HD, :] for j in range(3)]
        rows = rows + [d_ctx[m * HD : (m + 1) * HD, :], id_rows]
        for u in range(2):
            for j, block in enumerate(rows):
                own[4 * u + m, j * HD : j * HD + block.shape[0], :] = block


def attention_kernel(zz, local, halo, out, grads, win, kn, vn, idk, es, ds, ps, dss, gk, gv):
    u, m = lax.div(zz[0], 4), lax.rem(zz[0], 4)

    @pl.when(u == 0)
    def _():
        win[:3] = halo[...]
        win[3:] = local[:7]

    @pl.when(u == 1)
    def _():
        win[:7] = local[1:]
        win[7:] = halo[...]

    def rows(c, j):
        return win[c, j * HD : (j + 1) * HD, :]

    def side(first, last, j):
        return jnp.concatenate([rows(c, j) for c in range(first, last)], axis=1)

    ids = [win[c, 4 * HD : 4 * HD + 1, :].astype(F32) for c in range(WIN)]
    for c in range(WIN):
        at = slice(c * T, (c + 1) * T)
        idk[at, :] = jnp.transpose(jnp.broadcast_to(ids[c], (2 * T, T)))
        kn[at, :] = jnp.transpose(rows(c, 1))
        vn[at, :] = jnp.transpose(rows(c, 2))
    gk[...] = jnp.zeros(gk.shape, F32)
    gv[...] = jnp.zeros(gv.shape, F32)
    for qa, qb, ka, kb in GROUPS:
        n = (qb - qa) * T
        qt, dt = side(qa, qb, 0), side(qa, qb, 3)
        idq = jnp.concatenate(ids[qa:qb], axis=1)
        esum = jnp.zeros((1, n), F32)
        dsum = jnp.zeros((1, n), F32)
        for c in range(ka, kb):
            kr = slice(c * T, (c + 1) * T)
            s = jnp.dot(kn[kr, :], qt, preferred_element_type=F32)
            dp = jnp.dot(vn[kr, :], dt, preferred_element_type=F32)
            e = jnp.exp2(jnp.where(idk[kr, :] == idq, s * (SCALE * LOG2E), -1e30))
            es[kr, :] = e
            ds[kr, :] = dp
            esum = esum + jnp.sum(e, axis=0, keepdims=True)
            dsum = dsum + jnp.sum(e * dp, axis=0, keepdims=True)
        r = 1.0 / jnp.maximum(esum, 1e-37)
        delta = dsum * r
        qs, qe = max(qa, OWN), min(qb, OWN + 4)
        ks, ke = max(ka, OWN), min(kb, OWN + 4)
        for c in range(ka, kb) if qs < qe else range(ks, ke):
            kr = slice(c * T, (c + 1) * T)
            p = es[kr, :] * r
            ps[kr, :] = p.astype(BF16)
            dss[kr, :] = (p * (ds[kr, :] - delta)).astype(BF16)
        own = slice(ks * T, ke * T)
        to = slice((ks - OWN) * T, (ke - OWN) * T)
        gk[:, to] += lax.dot_general(qt, dss[own, :], LANES, preferred_element_type=F32)
        gv[:, to] += lax.dot_general(dt, ps[own, :], LANES, preferred_element_type=F32)
        if qs < qe:
            cols = slice((qs - qa) * T, (qe - qa) * T)
            kr = slice(ka * T, kb * T)
            gq = jnp.dot(side(ka, kb, 1), dss[kr, cols], preferred_element_type=F32) * SCALE
            ctx = jnp.dot(side(ka, kb, 2), ps[kr, cols], preferred_element_type=F32)
            for i in range(qe - qs):
                lane = slice(i * T, (i + 1) * T)
                grads[qs - OWN + i, :HD, :] = gq[:, lane].astype(BF16)
                grads[qs - OWN + i, 3 * HD :, :] = ctx[:, lane].astype(BF16)
    for i in range(4):
        lane = slice(i * T, (i + 1) * T)
        grads[i, HD : 2 * HD, :] = (gk[:, lane] * SCALE).astype(BF16)
        grads[i, 2 * HD : 3 * HD, :] = gv[:, lane].astype(BF16)
    for k in range(4):
        out[k] = grads[jnp.bitwise_xor(m, k)]


def attention(zz, local, halo):
    big = (WIN * T, 2 * T)
    return call(
        attention_kernel,
        "attention",
        shape((4, 4 * HD, T)),
        [
            pltpu.VMEM((4, 4 * HD, T), BF16),
            pltpu.VMEM((WIN, R, T), BF16),
            pltpu.VMEM((WIN * T, HD), BF16),
            pltpu.VMEM((WIN * T, HD), BF16),
            pltpu.VMEM(big, F32),
            pltpu.VMEM(big, F32),
            pltpu.VMEM(big, F32),
            pltpu.VMEM(big, BF16),
            pltpu.VMEM(big, BF16),
            pltpu.VMEM((HD, 4 * T), F32),
            pltpu.VMEM((HD, 4 * T), F32),
        ],
        [zz],
        local,
        halo,
    )


def pieces_kernel(zz, head, b0, b1, b2, b3, proj, w, w_out, out, grads, parts):
    m = lax.rem(zz[0], 4)
    for k, piece in enumerate((b0, b1, b2, b3)):
        other = jnp.bitwise_xor(m, k)
        for j in range(4):
            grads[times(j * HL + other, HD), :] = piece[j * HD : (j + 1) * HD, :]
    total = jnp.sum(grads[: 3 * W, :].astype(F32) * proj[...].astype(F32), axis=0, keepdims=True)
    hi = total.astype(BF16).astype(F32)
    row = lax.broadcasted_iota(jnp.int32, (IDROWS, T), 0)
    tail = jnp.where(row == 0, hi, jnp.where(row == 1, total - hi, 0.0)).astype(BF16)
    g = jnp.transpose(grads[...])
    d_part = jnp.dot(g[:, : 3 * W], w[...], preferred_element_type=F32)
    out_part = jnp.dot(g[:, 3 * W :], w_out[...], preferred_element_type=F32)
    out_part = jnp.transpose(out_part.astype(BF16))
    d_part = jnp.transpose(d_part.astype(BF16))
    for j in range(4):
        parts[j, :W, :] = out_part[j * W : (j + 1) * W, :]
        parts[j, W : 2 * W, :] = d_part[j * W : (j + 1) * W, :]
        parts[j, 2 * W :, :] = tail
    for k in range(4):
        out[k] = parts[jnp.bitwise_xor(head[0], k)]


def rows_kernel(g0, g1, g2, g3, x_own, scale_own, inv, attn_out, grad_patches):
    total = g0[...].astype(F32) + g1[...].astype(F32) + g2[...].astype(F32) + g3[...].astype(F32)
    attn_out[...] = total[:W, :].astype(BF16)
    d_own = total[W : 2 * W, :]
    x = x_own[...].astype(F32)
    i = inv[0:1, :]
    row_total = total[2 * W : 2 * W + 1, :] + total[2 * W + 1 : 2 * W + 2, :]
    grad_patches[...] = (scale_own[...] * d_own - x * (i * i * row_total * (1.0 / D))).astype(BF16)


def assemble_kernel(head, h0, h1, h2, h3, n, c):
    for j, quarter in enumerate((h0, h1, h2, h3)):
        at = times(jnp.bitwise_xor(head[0], j), W)
        for k in range(4):
            lane = slice(k * T, (k + 1) * T)
            n[at, lane] = quarter[2 * k * W : (2 * k + 1) * W, :]
            c[at, lane] = quarter[(2 * k + 1) * W : (2 * k + 2) * W, :]


def weights_kernel(zz, n, c, grads, w, out, g, term):
    m = lax.rem(zz[0], 4)
    for k in range(4):
        g[:, k * T : (k + 1) * T] = grads[k]
    left = lax.dot_general(n[...], g[: 3 * HD, :], LANES, preferred_element_type=F32)
    right = lax.dot_general(c[...], g[3 * HD :, :], LANES, preferred_element_type=F32)
    term[...] = jnp.concatenate([left, right], axis=1)
    turned = lax.dot_general(g[: 3 * HD, :], n[...], LANES, preferred_element_type=F32)
    gg = jnp.zeros((1, D), F32)
    for j in range(3):
        product = turned[j * HD : (j + 1) * HD, :] * w[times(j * HL + m, HD), :].astype(F32)
        gg = gg + jnp.sum(product, axis=0, keepdims=True)
    rows = [gg[:, l * T : (l + 1) * T] for l in range(10)]
    rows = rows + [jnp.zeros((6, T), F32)]
    tail = jnp.concatenate(rows, axis=0).astype(BF16)
    for d in range(8):
        out[d, :160, :] = term[160 * d : 160 * d + 160, :T].astype(BF16)
        out[d, 160:320, :] = term[160 * d : 160 * d + 160, T : 2 * T].astype(BF16)
        halves = [term[160 * d + 80 * i : 160 * d + 80 * i + 80, 2 * T :] for i in range(2)]
        out[d, 320:400, :] = jnp.concatenate(halves, axis=1).astype(BF16)
        out[d, 400:, :] = tail


def middle_kernel(got, out, total):
    total[...] = sum(got[i].astype(F32) for i in range(8))
    zero = jnp.zeros((4, T), F32)
    for z in range(8):
        third = total[320 + 20 * (z % 4) : 340 + 20 * (z % 4), :]
        if z >= 4:
            third = pltpu.roll(third, 64, 1)
        rows = [total[20 * z : 20 * z + 20, :], total[160 + 20 * z : 180 + 20 * z, :], third]
        out[7 - z] = jnp.concatenate(rows + [zero, total[400:, :]], axis=0).astype(BF16)


def sums_kernel(got, qkv, out, gg):
    tail = jnp.zeros((16, T), F32)
    cols = []
    for m in range(HL):
        total = got[7 - m].astype(F32) + got[3 - m].astype(F32)
        cols.append(jnp.concatenate([total[20 * l : 20 * l + 20, :] for l in range(3)], axis=1))
        tail = tail + total[64:80, :]
    for j in range(3):
        qkv[j] = jnp.concatenate([x[:, j * HD : (j + 1) * HD] for x in cols], axis=1)
    out[...] = jnp.concatenate([x[:, 3 * HD : 4 * HD] for x in cols], axis=1)
    gg[...] = tail


def gain_kernel(head, t0, t1, t2, t3, gain, out):
    total = (t0[...] + t1[...] + t2[...] + t3[...])[:10, :] / gain[...]
    flat = jnp.concatenate([total[l : l + 1, :] for l in range(10)], axis=1)
    for j in range(4):
        @pl.when(head[0] == j)
        def _():
            out[...] = flat[0, j * W : (j + 1) * W]


def along_z(x, by):
    return lax.ppermute(x, "z", [(i, i ^ by) for i in range(8)]) if by else x


def along_head(x, by):
    return lax.ppermute(x, HEAD, [(i, i ^ by) for i in range(4)]) if by else x


def to_next_group(x):
    pairs = []
    for i in range(64):
        group = i // 8 + (1 if i % 8 < 4 else -1)
        if 0 <= group < 8:
            pairs.append((i, group * 8 + i % 8))
    return lax.ppermute(x, SEQ, pairs)


def body(patches, gain, w_qkv, w_out, image_ids, cotangent):
    head = lax.axis_index(HEAD).astype(jnp.int32).reshape(1)
    zz = lax.axis_index("z").astype(jnp.int32).reshape(1)
    cot = cotangent.T
    gain = gain.reshape(10, T)
    w = w_qkv.transpose(1, 2, 0).reshape(3 * W, D)
    normed, quarter, x_own, scale_own, inv = call(
        norm_kernel,
        "norm",
        [shape((D, T)), shape((2 * W, T)), shape((W, T)), shape((W, T), F32), shape((8, T), F32)],
        [
            pltpu.VMEM((T, D), BF16),
            pltpu.VMEM((10, T), F32),
            pltpu.VMEM((D, T), BF16),
            pltpu.VMEM((D, T), F32),
            pltpu.SemaphoreType.DMA((3,)),
        ],
        [head],
        patches,
        gain,
        cot,
        far=3,
        limit=60,
    )
    cot, normed = lax.optimization_barrier((cot, normed))
    cots = [along_head(cot, k) for k in range(4)]
    quarter = [quarter, along_z(quarter, 1), None, along_z(quarter, 3)]
    quarter[3], cots = lax.optimization_barrier((quarter[3], cots))
    quarter[2] = along_z(quarter[3], 1)
    quarter = jnp.concatenate(quarter, axis=0)
    ids = image_ids.reshape(1, T)
    proj = call(project_kernel, "project", shape((3 * W, T)), [], [], normed, w, w_out, ids)
    own = call(
        payload_kernel,
        "payload",
        shape((8, R, T)),
        [pltpu.VMEM((D, T), BF16)],
        [head],
        *cots,
        proj,
        w_out,
        ids,
    )
    own, quarter = lax.optimization_barrier((own, quarter))
    local = lax.all_to_all(own, "z", 0, 0, tiled=True)
    near = lax.dynamic_slice_in_dim(local, jnp.where(zz[0] < 4, 5, 0), 3, 0)
    across = along_head(quarter, 2)
    near, across = lax.optimization_barrier((near, across))
    halo = to_next_group(near)
    quarters = [quarter, along_head(quarter, 1), across, along_head(across, 1)]
    n, c = call(
        assemble_kernel, "assemble", [shape((D, 4 * T))] * 2, [], [head], *quarters
    )
    halo, n, c = lax.optimization_barrier((halo, n, c))
    grads = attention(zz, local, halo)
    backs = [grads[k] for k in range(4)]
    terms = call(
        weights_kernel,
        "weights",
        shape((8, 416, T)),
        [pltpu.VMEM((W, 4 * T), BF16), pltpu.VMEM((D, W), F32)],
        [zz],
        n,
        c,
        grads,
        w,
    )
    backs, terms = lax.optimization_barrier((backs, terms))
    terms = lax.all_to_all(terms, ("y", "xh"), 0, 0, tiled=True)
    backs = [along_z(b, k) for k, b in enumerate(backs)]
    pieces = call(
        pieces_kernel,
        "pieces",
        shape((4, 2 * W + IDROWS, T)),
        [pltpu.VMEM((4 * W, T), BF16), pltpu.VMEM((4, 2 * W + IDROWS, T), BF16)],
        [zz, head],
        *backs,
        proj,
        w,
        w_out,
    )
    terms, pieces = lax.optimization_barrier((terms, pieces))
    got = [along_head(pieces[k], k) for k in range(4)]
    terms = call(middle_kernel, "middle", shape((8, 80, T)), [pltpu.VMEM((416, T), F32)], [], terms)
    terms = lax.all_to_all(
        terms, "z", 0, 0, tiled=True, axis_index_groups=[list(range(7, -1, -1))]
    )
    attn_out, grad_patches = call(
        rows_kernel,
        "rows",
        [shape((W, T)), shape((W, T))],
        [],
        [],
        *got,
        x_own,
        scale_own,
        inv,
    )
    grad_w_qkv, grad_w_out, gg = call(
        sums_kernel,
        "sums",
        [shape((3, 20, W), F32), shape((20, W), F32), shape((16, T), F32)],
        [],
        [],
        terms,
    )
    grad_gain = call(
        gain_kernel, "gain", shape((W,), F32), [], [head], *[along_head(gg, k) for k in range(4)], gain
    )
    return (attn_out.T, grad_patches.T, grad_w_qkv.transpose(1, 0, 2), grad_w_out.T, grad_gain)


def solution(mesh):
    fine = Mesh(mesh.devices.reshape(4, 2, 8, 2, 2), SEQ + HEAD)
    in_specs = (
        P(SEQ, None),
        P(),
        P(None, None, HEAD),
        P(HEAD, None),
        P(SEQ),
        P(SEQ, HEAD),
    )
    out_specs = (
        P(SEQ, HEAD),
        P(SEQ, HEAD),
        P(SEQ, None, HEAD),
        P(HEAD, SEQ),
        P(HEAD),
    )
    return jax.shard_map(body, mesh=fine, in_specs=in_specs, out_specs=out_specs, check_vma=False)
```

```python
import jax
import jax.numpy as jnp
from jax import lax
from jax.experimental import pallas as pl
from jax.experimental.pallas import tpu as pltpu
from jax.sharding import Mesh, PartitionSpec as P

D = 1280
HD = 80
T = 128
HL = 4
W = HL * HD
IDROWS = 16
R = 4 * HD + IDROWS
WIN = 10
OWN = 3
SCALE = HD ** (-0.5)
LOG2E = 1.4426950408889634
SEQ = ("y", "xh", "z")
HEAD = ("xl", "c")
F32 = jnp.float32
BF16 = jnp.bfloat16
LANES = (((1,), (1,)), ((), ()))
GROUPS = ((0, 2, 0, 5), (2, 4, 0, 7), (4, 6, 1, 9), (6, 8, 3, 10), (8, 10, 5, 10))


def call(kernel, name, outs, scratch, scalars, *args, far=0, far_outs=0, limit=12):
    single = not isinstance(outs, (list, tuple))
    vmem, hbm = pl.BlockSpec(memory_space=pltpu.VMEM), pl.BlockSpec(memory_space=pltpu.HBM)
    specs = [pl.BlockSpec(memory_space=pltpu.SMEM)] * len(scalars)
    specs += [vmem] * (len(args) - far) + [hbm] * far
    return pl.pallas_call(
        kernel,
        out_shape=outs,
        in_specs=specs,
        out_specs=vmem if single else [vmem] * (len(outs) - far_outs) + [hbm] * far_outs,
        scratch_shapes=scratch,
        compiler_params=pltpu.CompilerParams(vmem_limit_bytes=limit * 1024 * 1024),
        cost_estimate=pl.CostEstimate(flops=1000, bytes_accessed=1000, transcendentals=0),
        name=name,
    )(*scalars, *args)


def fetch(sems, *pairs):
    copies = [pltpu.make_async_copy(src, dst, sems.at[i]) for i, (src, dst) in enumerate(pairs)]
    for copy in copies:
        copy.start()
    return copies


def shape(dims, dtype=BF16):
    return jax.ShapeDtypeStruct(dims, dtype)


def times(index, size):
    return pl.ds(pl.multiple_of(index * size, size), size)


def norm_kernel(head, patches_far, gain_far, cot_far, normed, quarter, x_own, scale_own, inv_out, patches, gain, xt, scale, sems):
    copies = fetch(sems, (patches_far, patches), (gain_far, gain), (cot_far, quarter.at[W:]))
    copies[0].wait()
    copies[1].wait()
    xt[...] = jnp.transpose(patches[...])
    x = xt[...].astype(F32)
    inv = lax.rsqrt(jnp.sum(x * x, axis=0, keepdims=True) * (1.0 / D) + 1e-06)
    for l in range(10):
        rows = slice(l * T, (l + 1) * T)
        g = jnp.transpose(jnp.broadcast_to(gain[l : l + 1, :], (T, T)))
        scale[rows, :] = inv * g
        normed[rows, :] = (xt[rows, :].astype(F32) * inv * g).astype(BF16)
    inv_out[...] = jnp.broadcast_to(inv, (8, T))
    at = times(head[0], W)
    x_own[...] = xt[at, :]
    scale_own[...] = scale[at, :]
    quarter[:W, :] = normed[at, :]
    copies[2].wait()


def project_kernel(normed, w, w_out, ids, proj):
    proj[...] = jnp.dot(w[...], normed[...], preferred_element_type=F32).astype(BF16)


def payload_kernel(head, zz, c0, c1, c2, c3, proj, w_out, ids, e0, e1, e2, e3, own, cot):
    for k, piece in enumerate((c0, c1, c2, c3)):
        cot[times(jnp.bitwise_xor(head[0], k), W), :] = piece[...]
    d_ctx = jnp.dot(w_out[...], cot[...], preferred_element_type=F32).astype(BF16)
    id_rows = jnp.broadcast_to((ids[...] + 1).astype(F32), (IDROWS, T)).astype(BF16)
    for m in range(HL):
        rows = [proj[j * W + m * HD : j * W + (m + 1) * HD, :] for j in range(3)]
        rows = rows + [d_ctx[m * HD : (m + 1) * HD, :], id_rows]
        for j, block in enumerate(rows):
            own[m, j * HD : j * HD + block.shape[0], :] = block
    m = lax.rem(zz[0], 4)
    for k, out in enumerate((e0, e1, e2, e3)):
        out[...] = own[jnp.bitwise_xor(m, k)]


def near_kernel(zz, r4, r5, r6, r7, out, far):
    for i, block in enumerate((r4, r5, r6, r7)):
        far[i] = block[...]
    first = jnp.where(zz[0] < 4, 5, 0)
    for i in range(3):
        out[i] = far[jnp.bitwise_xor(zz[0], first + i) - 4]


def attention_kernel(zz, r0, r1, r2, r3, r4, r5, r6, r7, halo, out, grads, win, kn, vn, idk, es, ds, ps, dss, gk, gv):
    u, m = lax.div(zz[0], 4), lax.rem(zz[0], 4)

    for k, block in enumerate((r0, r1, r2, r3, r4, r5, r6, r7)):
        win[jnp.bitwise_xor(zz[0], k) + jnp.where(u == 0, 4, 0)] = block[...]

    @pl.when(u == 0)
    def _():
        win[1:4] = halo[...]

    @pl.when(u == 1)
    def _():
        win[8:11] = halo[...]

    def rows(c, j):
        return win[1 + c, j * HD : (j + 1) * HD, :]

    def side(first, last, j):
        return jnp.concatenate([rows(c, j) for c in range(first, last)], axis=1)

    ids = [win[1 + c, 4 * HD : 4 * HD + 1, :].astype(F32) for c in range(WIN)]
    for c in range(WIN):
        at = slice(c * T, (c + 1) * T)
        idk[at, :] = jnp.transpose(jnp.broadcast_to(ids[c], (2 * T, T)))
        kn[at, :] = jnp.transpose(rows(c, 1))
        vn[at, :] = jnp.transpose(rows(c, 2))
    gk[...] = jnp.zeros(gk.shape, F32)
    gv[...] = jnp.zeros(gv.shape, F32)
    for qa, qb, ka, kb in GROUPS:
        n = (qb - qa) * T
        qt, dt = side(qa, qb, 0), side(qa, qb, 3)
        idq = jnp.concatenate(ids[qa:qb], axis=1)
        esum = jnp.zeros((1, n), F32)
        dsum = jnp.zeros((1, n), F32)
        for c in range(ka, kb):
            kr = slice(c * T, (c + 1) * T)
            s = jnp.dot(kn[kr, :], qt, preferred_element_type=F32)
            dp = jnp.dot(vn[kr, :], dt, preferred_element_type=F32)
            e = jnp.exp2(jnp.where(idk[kr, :] == idq, s * (SCALE * LOG2E), -1e30))
            es[kr, :] = e
            ds[kr, :] = dp
            esum = esum + jnp.sum(e, axis=0, keepdims=True)
            dsum = dsum + jnp.sum(e * dp, axis=0, keepdims=True)
        r = 1.0 / jnp.maximum(esum, 1e-37)
        delta = dsum * r
        qs, qe = max(qa, OWN), min(qb, OWN + 4)
        ks, ke = max(ka, OWN), min(kb, OWN + 4)
        for c in range(ka, kb) if qs < qe else range(ks, ke):
            kr = slice(c * T, (c + 1) * T)
            p = es[kr, :] * r
            ps[kr, :] = p.astype(BF16)
            dss[kr, :] = (p * (ds[kr, :] - delta)).astype(BF16)
        own = slice(ks * T, ke * T)
        to = slice((ks - OWN) * T, (ke - OWN) * T)
        gk[:, to] += lax.dot_general(qt, dss[own, :], LANES, preferred_element_type=F32)
        gv[:, to] += lax.dot_general(dt, ps[own, :], LANES, preferred_element_type=F32)
        if qs < qe:
            cols = slice((qs - qa) * T, (qe - qa) * T)
            kr = slice(ka * T, kb * T)
            gq = jnp.dot(side(ka, kb, 1), dss[kr, cols], preferred_element_type=F32) * SCALE
            ctx = jnp.dot(side(ka, kb, 2), ps[kr, cols], preferred_element_type=F32)
            for i in range(qe - qs):
                lane = slice(i * T, (i + 1) * T)
                grads[qs - OWN + i, :HD, :] = gq[:, lane].astype(BF16)
                grads[qs - OWN + i, 3 * HD :, :] = ctx[:, lane].astype(BF16)
    for i in range(4):
        lane = slice(i * T, (i + 1) * T)
        grads[i, HD : 2 * HD, :] = (gk[:, lane] * SCALE).astype(BF16)
        grads[i, 2 * HD : 3 * HD, :] = gv[:, lane].astype(BF16)
    for k in range(4):
        out[k] = grads[jnp.bitwise_xor(m, k)]


def attention(zz, locals_, halo):
    big = (WIN * T, 2 * T)
    return call(
        attention_kernel,
        "attention",
        shape((4, 4 * HD, T)),
        [
            pltpu.VMEM((4, 4 * HD, T), BF16),
            pltpu.VMEM((WIN + 2, R, T), BF16),
            pltpu.VMEM((WIN * T, HD), BF16),
            pltpu.VMEM((WIN * T, HD), BF16),
            pltpu.VMEM(big, F32),
            pltpu.VMEM(big, F32),
            pltpu.VMEM(big, F32),
            pltpu.VMEM(big, BF16),
            pltpu.VMEM(big, BF16),
            pltpu.VMEM((HD, 4 * T), F32),
            pltpu.VMEM((HD, 4 * T), F32),
        ],
        [zz],
        *locals_,
        halo,
    )


def pieces_kernel(zz, head, b0, b1, b2, b3, proj, w, w_out, out, grads, parts):
    m = lax.rem(zz[0], 4)
    for k, piece in enumerate((b0, b1, b2, b3)):
        other = jnp.bitwise_xor(m, k)
        for j in range(4):
            grads[times(j * HL + other, HD), :] = piece[j * HD : (j + 1) * HD, :]
    total = jnp.sum(grads[: 3 * W, :].astype(F32) * proj[...].astype(F32), axis=0, keepdims=True)
    hi = total.astype(BF16).astype(F32)
    row = lax.broadcasted_iota(jnp.int32, (IDROWS, T), 0)
    tail = jnp.where(row == 0, hi, jnp.where(row == 1, total - hi, 0.0)).astype(BF16)
    g = jnp.transpose(grads[...])
    d_part = jnp.dot(g[:, : 3 * W], w[...], preferred_element_type=F32)
    out_part = jnp.dot(g[:, 3 * W :], w_out[...], preferred_element_type=F32)
    out_part = jnp.transpose(out_part.astype(BF16))
    d_part = jnp.transpose(d_part.astype(BF16))
    for j in range(4):
        parts[j, :W, :] = out_part[j * W : (j + 1) * W, :]
        parts[j, W : 2 * W, :] = d_part[j * W : (j + 1) * W, :]
        parts[j, 2 * W :, :] = tail
    for k in range(4):
        out[k] = parts[jnp.bitwise_xor(head[0], k)]


def rows_kernel(g0, g1, g2, g3, x_own, scale_own, inv, attn_out, grad_patches):
    total = g0[...].astype(F32) + g1[...].astype(F32) + g2[...].astype(F32) + g3[...].astype(F32)
    attn_out[...] = total[:W, :].astype(BF16)
    d_own = total[W : 2 * W, :]
    x = x_own[...].astype(F32)
    i = inv[0:1, :]
    row_total = total[2 * W : 2 * W + 1, :] + total[2 * W + 1 : 2 * W + 2, :]
    grad_patches[...] = (scale_own[...] * d_own - x * (i * i * row_total * (1.0 / D))).astype(BF16)


def assemble_kernel(head, *refs):
    n, c = refs[8:]
    for j in range(4):
        at = times(jnp.bitwise_xor(head[0], j), W)
        for k, (part, row) in enumerate(((0, 0), (0, 1), (4, 0), (0, 2))):
            lane = slice(k * T, (k + 1) * T)
            n[at, lane] = refs[part + j][2 * row * W : (2 * row + 1) * W, :]
            c[at, lane] = refs[part + j][(2 * row + 1) * W : (2 * row + 2) * W, :]


def weights_kernel(zz, n, c, grads, w, out, g, term):
    m = lax.rem(zz[0], 4)
    for k in range(4):
        g[:, k * T : (k + 1) * T] = grads[k]
    left = lax.dot_general(n[...], g[: 3 * HD, :], LANES, preferred_element_type=F32)
    right = lax.dot_general(c[...], g[3 * HD :, :], LANES, preferred_element_type=F32)
    term[...] = jnp.concatenate([left, right], axis=1)
    turned = lax.dot_general(g[: 3 * HD, :], n[...], LANES, preferred_element_type=F32)
    gg = jnp.zeros((1, D), F32)
    for j in range(3):
        product = turned[j * HD : (j + 1) * HD, :] * w[times(j * HL + m, HD), :].astype(F32)
        gg = gg + jnp.sum(product, axis=0, keepdims=True)
    rows = [gg[:, l * T : (l + 1) * T] for l in range(10)]
    rows = rows + [jnp.zeros((6, T), F32)]
    tail = jnp.concatenate(rows, axis=0).astype(BF16)
    for d in range(8):
        out[d, :160, :] = term[160 * d : 160 * d + 160, :T].astype(BF16)
        out[d, 160:320, :] = term[160 * d : 160 * d + 160, T : 2 * T].astype(BF16)
        halves = [term[160 * d + 80 * i : 160 * d + 80 * i + 80, 2 * T :] for i in range(2)]
        out[d, 320:400, :] = jnp.concatenate(halves, axis=1).astype(BF16)
        out[d, 400:, :] = tail


def middle_kernel(got, out, total):
    total[...] = sum(got[i].astype(F32) for i in range(8))
    zero = jnp.zeros((4, T), F32)
    for z in range(8):
        third = total[320 + 20 * (z % 4) : 340 + 20 * (z % 4), :]
        if z >= 4:
            third = pltpu.roll(third, 64, 1)
        rows = [total[20 * z : 20 * z + 20, :], total[160 + 20 * z : 180 + 20 * z, :], third]
        out[7 - z] = jnp.concatenate(rows + [zero, total[400:, :]], axis=0).astype(BF16)


def sums_kernel(got, qkv, out, gg):
    tail = jnp.zeros((16, T), F32)
    cols = []
    for m in range(HL):
        total = got[7 - m].astype(F32) + got[3 - m].astype(F32)
        cols.append(jnp.concatenate([total[20 * l : 20 * l + 20, :] for l in range(3)], axis=1))
        tail = tail + total[64:80, :]
    for j in range(3):
        qkv[j] = jnp.concatenate([x[:, j * HD : (j + 1) * HD] for x in cols], axis=1)
    out[...] = jnp.concatenate([x[:, 3 * HD : 4 * HD] for x in cols], axis=1)
    gg[...] = tail


def gain_kernel(head, t0, t1, t2, t3, gain, out):
    total = (t0[...] + t1[...] + t2[...] + t3[...])[:10, :] / gain[...]
    flat = jnp.concatenate([total[l : l + 1, :] for l in range(10)], axis=1)
    for j in range(4):
        @pl.when(head[0] == j)
        def _():
            out[...] = flat[0, j * W : (j + 1) * W]


def along_z(x, by):
    return lax.ppermute(x, "z", [(i, i ^ by) for i in range(8)]) if by else x


def along_head(x, by):
    return lax.ppermute(x, HEAD, [(i, i ^ by) for i in range(4)]) if by else x


def to_next_group(x):
    pairs = []
    for i in range(64):
        group = i // 8 + (1 if i % 8 < 4 else -1)
        if 0 <= group < 8:
            pairs.append((i, group * 8 + i % 8))
    return lax.ppermute(x, SEQ, pairs)


def body(patches, gain, w_qkv, w_out, image_ids, cotangent):
    head = lax.axis_index(HEAD).astype(jnp.int32).reshape(1)
    zz = lax.axis_index("z").astype(jnp.int32).reshape(1)
    cot = cotangent.T
    gain = gain.reshape(10, T)
    w = w_qkv.transpose(1, 2, 0).reshape(3 * W, D)
    normed, quarter, x_own, scale_own, inv = call(
        norm_kernel,
        "norm",
        [shape((D, T)), shape((2 * W, T)), shape((W, T)), shape((W, T), F32), shape((8, T), F32)],
        [
            pltpu.VMEM((T, D), BF16),
            pltpu.VMEM((10, T), F32),
            pltpu.VMEM((D, T), BF16),
            pltpu.VMEM((D, T), F32),
            pltpu.SemaphoreType.DMA((3,)),
        ],
        [head],
        patches,
        gain,
        cot,
        far=3,
        limit=60,
    )
    cot, normed = lax.optimization_barrier((cot, normed))
    cots = [along_head(cot, k) for k in range(4)]
    quarter = [quarter, along_z(quarter, 1), None, along_z(quarter, 3)]
    ids = image_ids.reshape(1, T)
    proj = call(project_kernel, "project", shape((3 * W, T)), [], [], normed, w, w_out, ids)
    own = call(
        payload_kernel,
        "payload",
        [shape((R, T))] * 4,
        [pltpu.VMEM((4, R, T), BF16), pltpu.VMEM((D, T), BF16)],
        [head, zz],
        *cots,
        proj,
        w_out,
        ids,
    )
    own, quarter[1], quarter[3] = lax.optimization_barrier((own, quarter[1], quarter[3]))
    local = {k: along_z(own[k % 4], k) for k in (4, 5, 6, 7, 0, 1, 2, 3)}
    first = jnp.concatenate([quarter[0], quarter[1], quarter[3]], axis=0)
    last = along_z(quarter[3], 1)
    near = call(
        near_kernel,
        "near",
        shape((3, R, T)),
        [pltpu.VMEM((4, R, T), BF16)],
        [zz],
        *[local[k] for k in (4, 5, 6, 7)],
    )
    across = along_head(first, 2)
    near, local[2], local[3] = lax.optimization_barrier((near, local[2], local[3]))
    halo = to_next_group(near)
    quarters = [first, along_head(first, 1), across, along_head(across, 1)]
    across = along_head(last, 2)
    quarters += [last, along_head(last, 1), across, along_head(across, 1)]
    n, c = call(
        assemble_kernel, "assemble", [shape((D, 4 * T))] * 2, [], [head], *quarters
    )
    grads = attention(zz, [local[k] for k in range(8)], halo)
    backs = [grads[k] for k in range(4)]
    terms = call(
        weights_kernel,
        "weights",
        shape((8, 416, T)),
        [pltpu.VMEM((W, 4 * T), BF16), pltpu.VMEM((D, W), F32)],
        [zz],
        n,
        c,
        grads,
        w,
    )
    backs, terms = lax.optimization_barrier((backs, terms))
    terms = lax.all_to_all(terms, ("y", "xh"), 0, 0, tiled=True)
    backs = [along_z(b, k) for k, b in enumerate(backs)]
    pieces = call(
        pieces_kernel,
        "pieces",
        shape((4, 2 * W + IDROWS, T)),
        [pltpu.VMEM((4 * W, T), BF16), pltpu.VMEM((4, 2 * W + IDROWS, T), BF16)],
        [zz, head],
        *backs,
        proj,
        w,
        w_out,
    )
    terms, pieces = lax.optimization_barrier((terms, pieces))
    got = [along_head(pieces[k], k) for k in range(4)]
    terms = call(middle_kernel, "middle", shape((8, 80, T)), [pltpu.VMEM((416, T), F32)], [], terms)
    terms = lax.all_to_all(
        terms, "z", 0, 0, tiled=True, axis_index_groups=[list(range(7, -1, -1))]
    )
    attn_out, grad_patches = call(
        rows_kernel,
        "rows",
        [shape((W, T)), shape((W, T))],
        [],
        [],
        *got,
        x_own,
        scale_own,
        inv,
    )
    grad_w_qkv, grad_w_out, gg = call(
        sums_kernel,
        "sums",
        [shape((3, 20, W), F32), shape((20, W), F32), shape((16, T), F32)],
        [],
        [],
        terms,
    )
    grad_gain = call(
        gain_kernel, "gain", shape((W,), F32), [], [head], *[along_head(gg, k) for k in range(4)], gain
    )
    return (attn_out.T, grad_patches.T, grad_w_qkv.transpose(1, 0, 2), grad_w_out.T, grad_gain)


def solution(mesh):
    fine = Mesh(mesh.devices.reshape(4, 2, 8, 2, 2), SEQ + HEAD)
    in_specs = (
        P(SEQ, None),
        P(),
        P(None, None, HEAD),
        P(HEAD, None),
        P(SEQ),
        P(SEQ, HEAD),
    )
    out_specs = (
        P(SEQ, HEAD),
        P(SEQ, HEAD),
        P(SEQ, None, HEAD),
        P(HEAD, SEQ),
        P(HEAD),
    )
    return jax.shard_map(body, mesh=fine, in_specs=in_specs, out_specs=out_specs, check_vma=False)
```

```python
import jax
import jax.numpy as jnp
from jax import lax
from jax.experimental import pallas as pl
from jax.experimental.pallas import tpu as pltpu
from jax.sharding import Mesh, PartitionSpec as P

D = 1280
HD = 80
T = 128
HL = 4
W = HL * HD
IDROWS = 16
R = 4 * HD + IDROWS
WIN = 10
OWN = 3
SCALE = HD ** (-0.5)
LOG2E = 1.4426950408889634
SEQ = ("y", "xh", "z")
HEAD = ("xl", "c")
F32 = jnp.float32
BF16 = jnp.bfloat16
LANES = (((1,), (1,)), ((), ()))
GROUPS = ((0, 2, 0, 5), (2, 4, 0, 7), (4, 6, 1, 9), (6, 8, 3, 10), (8, 10, 5, 10))


def call(kernel, name, outs, scratch, scalars, *args, far=0, far_outs=0, limit=12):
    single = not isinstance(outs, (list, tuple))
    vmem, hbm = pl.BlockSpec(memory_space=pltpu.VMEM), pl.BlockSpec(memory_space=pltpu.HBM)
    specs = [pl.BlockSpec(memory_space=pltpu.SMEM)] * len(scalars)
    specs += [vmem] * (len(args) - far) + [hbm] * far
    return pl.pallas_call(
        kernel,
        out_shape=outs,
        in_specs=specs,
        out_specs=vmem if single else [vmem] * (len(outs) - far_outs) + [hbm] * far_outs,
        scratch_shapes=scratch,
        compiler_params=pltpu.CompilerParams(vmem_limit_bytes=limit * 1024 * 1024),
        cost_estimate=pl.CostEstimate(flops=1000, bytes_accessed=1000, transcendentals=0),
        name=name,
    )(*scalars, *args)


def fetch(sems, *pairs):
    copies = [pltpu.make_async_copy(src, dst, sems.at[i]) for i, (src, dst) in enumerate(pairs)]
    for copy in copies:
        copy.start()
    return copies


def shape(dims, dtype=BF16):
    return jax.ShapeDtypeStruct(dims, dtype)


def times(index, size):
    return pl.ds(pl.multiple_of(index * size, size), size)


def norm_kernel(head, patches_far, gain_far, cot_far, normed, quarter, x_own, scale_own, inv_out, patches, gain, xt, scale, sems):
    copies = fetch(sems, (patches_far, patches), (gain_far, gain), (cot_far, quarter.at[W:]))
    copies[0].wait()
    copies[1].wait()
    xt[...] = jnp.transpose(patches[...])
    x = xt[...].astype(F32)
    inv = lax.rsqrt(jnp.sum(x * x, axis=0, keepdims=True) * (1.0 / D) + 1e-06)
    for l in range(10):
        rows = slice(l * T, (l + 1) * T)
        g = jnp.transpose(jnp.broadcast_to(gain[l : l + 1, :], (T, T)))
        scale[rows, :] = inv * g
        normed[rows, :] = (xt[rows, :].astype(F32) * inv * g).astype(BF16)
    inv_out[...] = jnp.broadcast_to(inv, (8, T))
    at = times(head[0], W)
    x_own[...] = xt[at, :]
    scale_own[...] = scale[at, :]
    quarter[:W, :] = normed[at, :]
    copies[2].wait()


def project_kernel(normed, w, proj):
    proj[...] = jnp.dot(w[...], normed[...], preferred_element_type=F32).astype(BF16)


def payload_kernel(head, zz, c0, c1, c2, c3, proj, w_out, ids, e0, e1, e2, e3, own, cot):
    for k, piece in enumerate((c0, c1, c2, c3)):
        cot[times(jnp.bitwise_xor(head[0], k), W), :] = piece[...]
    d_ctx = jnp.dot(w_out[...], cot[...], preferred_element_type=F32).astype(BF16)
    id_rows = jnp.broadcast_to((ids[...] + 1).astype(F32), (IDROWS, T)).astype(BF16)
    for m in range(HL):
        rows = [proj[j * W + m * HD : j * W + (m + 1) * HD, :] for j in range(3)]
        rows = rows + [d_ctx[m * HD : (m + 1) * HD, :], id_rows]
        for j, block in enumerate(rows):
            own[m, j * HD : j * HD + block.shape[0], :] = block
    m = lax.rem(zz[0], 4)
    for k, out in enumerate((e0, e1, e2, e3)):
        out[...] = own[jnp.bitwise_xor(m, k)]


def near_kernel(zz, r4, r5, r6, r7, out, far):
    for i, block in enumerate((r4, r5, r6, r7)):
        far[i] = block[...]
    first = jnp.where(zz[0] < 4, 5, 0)
    for i in range(3):
        out[i] = far[jnp.bitwise_xor(zz[0], first + i) - 4]


def attention_kernel(zz, r0, r1, r2, r3, r4, r5, r6, r7, halo, out, grads, win, kn, vn, idk, es, ds, ps, dss, gk, gv):
    u, m = lax.div(zz[0], 4), lax.rem(zz[0], 4)

    for k, block in enumerate((r0, r1, r2, r3, r4, r5, r6, r7)):
        win[jnp.bitwise_xor(zz[0], k) + jnp.where(u == 0, 4, 0)] = block[...]

    @pl.when(u == 0)
    def _():
        win[1:4] = halo[...]

    @pl.when(u == 1)
    def _():
        win[8:11] = halo[...]

    def rows(c, j):
        return win[1 + c, j * HD : (j + 1) * HD, :]

    def side(first, last, j):
        return jnp.concatenate([rows(c, j) for c in range(first, last)], axis=1)

    ids = [win[1 + c, 4 * HD : 4 * HD + 1, :].astype(F32) for c in range(WIN)]
    for c in range(WIN):
        at = slice(c * T, (c + 1) * T)
        idk[at, :] = jnp.transpose(jnp.broadcast_to(ids[c], (2 * T, T)))
        kn[at, :] = jnp.transpose(rows(c, 1))
        vn[at, :] = jnp.transpose(rows(c, 2))
    gk[...] = jnp.zeros(gk.shape, F32)
    gv[...] = jnp.zeros(gv.shape, F32)
    for qa, qb, ka, kb in GROUPS:
        n = (qb - qa) * T
        qt, dt = side(qa, qb, 0), side(qa, qb, 3)
        idq = jnp.concatenate(ids[qa:qb], axis=1)
        esum = jnp.zeros((1, n), F32)
        dsum = jnp.zeros((1, n), F32)
        for c in range(ka, kb):
            kr = slice(c * T, (c + 1) * T)
            s = jnp.dot(kn[kr, :], qt, preferred_element_type=F32)
            dp = jnp.dot(vn[kr, :], dt, preferred_element_type=F32)
            e = jnp.exp2(jnp.where(idk[kr, :] == idq, s * (SCALE * LOG2E), -1e30))
            es[kr, :] = e
            ds[kr, :] = dp
            esum = esum + jnp.sum(e, axis=0, keepdims=True)
            dsum = dsum + jnp.sum(e * dp, axis=0, keepdims=True)
        r = 1.0 / jnp.maximum(esum, 1e-37)
        delta = dsum * r
        qs, qe = max(qa, OWN), min(qb, OWN + 4)
        ks, ke = max(ka, OWN), min(kb, OWN + 4)
        for c in range(ka, kb) if qs < qe else range(ks, ke):
            kr = slice(c * T, (c + 1) * T)
            p = es[kr, :] * r
            ps[kr, :] = p.astype(BF16)
            dss[kr, :] = (p * (ds[kr, :] - delta)).astype(BF16)
        own = slice(ks * T, ke * T)
        to = slice((ks - OWN) * T, (ke - OWN) * T)
        gk[:, to] += lax.dot_general(qt, dss[own, :], LANES, preferred_element_type=F32)
        gv[:, to] += lax.dot_general(dt, ps[own, :], LANES, preferred_element_type=F32)
        if qs < qe:
            cols = slice((qs - qa) * T, (qe - qa) * T)
            kr = slice(ka * T, kb * T)
            gq = jnp.dot(side(ka, kb, 1), dss[kr, cols], preferred_element_type=F32) * SCALE
            ctx = jnp.dot(side(ka, kb, 2), ps[kr, cols], preferred_element_type=F32)
            for i in range(qe - qs):
                lane = slice(i * T, (i + 1) * T)
                grads[qs - OWN + i, :HD, :] = gq[:, lane].astype(BF16)
                grads[qs - OWN + i, 3 * HD :, :] = ctx[:, lane].astype(BF16)
    for i in range(4):
        lane = slice(i * T, (i + 1) * T)
        grads[i, HD : 2 * HD, :] = (gk[:, lane] * SCALE).astype(BF16)
        grads[i, 2 * HD : 3 * HD, :] = gv[:, lane].astype(BF16)
    for k in range(4):
        out[k] = grads[jnp.bitwise_xor(m, k)]


def attention(zz, locals_, halo):
    big = (WIN * T, 2 * T)
    return call(
        attention_kernel,
        "attention",
        shape((4, 4 * HD, T)),
        [
            pltpu.VMEM((4, 4 * HD, T), BF16),
            pltpu.VMEM((WIN + 2, R, T), BF16),
            pltpu.VMEM((WIN * T, HD), BF16),
            pltpu.VMEM((WIN * T, HD), BF16),
            pltpu.VMEM(big, F32),
            pltpu.VMEM(big, F32),
            pltpu.VMEM(big, F32),
            pltpu.VMEM(big, BF16),
            pltpu.VMEM(big, BF16),
            pltpu.VMEM((HD, 4 * T), F32),
            pltpu.VMEM((HD, 4 * T), F32),
        ],
        [zz],
        *locals_,
        halo,
    )


def pieces_kernel(zz, head, b0, b1, b2, b3, proj, w, w_out, out, grads, parts):
    m = lax.rem(zz[0], 4)
    for k, piece in enumerate((b0, b1, b2, b3)):
        other = jnp.bitwise_xor(m, k)
        for j in range(4):
            grads[times(j * HL + other, HD), :] = piece[j * HD : (j + 1) * HD, :]
    total = jnp.sum(grads[: 3 * W, :].astype(F32) * proj[...].astype(F32), axis=0, keepdims=True)
    hi = total.astype(BF16).astype(F32)
    row = lax.broadcasted_iota(jnp.int32, (IDROWS, T), 0)
    tail = jnp.where(row == 0, hi, jnp.where(row == 1, total - hi, 0.0)).astype(BF16)
    g = jnp.transpose(grads[...])
    d_part = jnp.dot(g[:, : 3 * W], w[...], preferred_element_type=F32)
    out_part = jnp.dot(g[:, 3 * W :], w_out[...], preferred_element_type=F32)
    out_part = jnp.transpose(out_part.astype(BF16))
    d_part = jnp.transpose(d_part.astype(BF16))
    for j in range(4):
        parts[j, :W, :] = out_part[j * W : (j + 1) * W, :]
        parts[j, W : 2 * W, :] = d_part[j * W : (j + 1) * W, :]
        parts[j, 2 * W :, :] = tail
    for k in range(4):
        out[k] = parts[jnp.bitwise_xor(head[0], k)]


def rows_kernel(g0, g1, g2, g3, x_own, scale_own, inv, attn_out, grad_patches):
    total = g0[...].astype(F32) + g1[...].astype(F32) + g2[...].astype(F32) + g3[...].astype(F32)
    attn_out[...] = total[:W, :].astype(BF16)
    d_own = total[W : 2 * W, :]
    x = x_own[...].astype(F32)
    i = inv[0:1, :]
    row_total = total[2 * W : 2 * W + 1, :] + total[2 * W + 1 : 2 * W + 2, :]
    grad_patches[...] = (scale_own[...] * d_own - x * (i * i * row_total * (1.0 / D))).astype(BF16)


def assemble_kernel(head, *refs):
    n, c = refs[8:]
    for j in range(4):
        at = times(jnp.bitwise_xor(head[0], j), W)
        for k, (part, row) in enumerate(((0, 0), (0, 1), (4, 0), (0, 2))):
            lane = slice(k * T, (k + 1) * T)
            n[at, lane] = refs[part + j][2 * row * W : (2 * row + 1) * W, :]
            c[at, lane] = refs[part + j][(2 * row + 1) * W : (2 * row + 2) * W, :]


def weights_kernel(zz, n, c, grads, w, out, g, term):
    m = lax.rem(zz[0], 4)
    for k in range(4):
        g[:, k * T : (k + 1) * T] = grads[k]
    left = lax.dot_general(n[...], g[: 3 * HD, :], LANES, preferred_element_type=F32)
    right = lax.dot_general(c[...], g[3 * HD :, :], LANES, preferred_element_type=F32)
    term[...] = jnp.concatenate([left, right], axis=1)
    turned = lax.dot_general(g[: 3 * HD, :], n[...], LANES, preferred_element_type=F32)
    gg = jnp.zeros((1, D), F32)
    for j in range(3):
        product = turned[j * HD : (j + 1) * HD, :] * w[times(j * HL + m, HD), :].astype(F32)
        gg = gg + jnp.sum(product, axis=0, keepdims=True)
    rows = [gg[:, l * T : (l + 1) * T] for l in range(10)]
    rows = rows + [jnp.zeros((6, T), F32)]
    tail = jnp.concatenate(rows, axis=0).astype(BF16)
    for d in range(8):
        out[d, :160, :] = term[160 * d : 160 * d + 160, :T].astype(BF16)
        out[d, 160:320, :] = term[160 * d : 160 * d + 160, T : 2 * T].astype(BF16)
        halves = [term[160 * d + 80 * i : 160 * d + 80 * i + 80, 2 * T :] for i in range(2)]
        out[d, 320:400, :] = jnp.concatenate(halves, axis=1).astype(BF16)
        out[d, 400:, :] = tail


def middle_kernel(got, out, total):
    total[...] = sum(got[i].astype(F32) for i in range(8))
    zero = jnp.zeros((4, T), F32)
    for z in range(8):
        third = total[320 + 20 * (z % 4) : 340 + 20 * (z % 4), :]
        if z >= 4:
            third = pltpu.roll(third, 64, 1)
        rows = [total[20 * z : 20 * z + 20, :], total[160 + 20 * z : 180 + 20 * z, :], third]
        out[7 - z] = jnp.concatenate(rows + [zero, total[400:, :]], axis=0).astype(BF16)


def tails_kernel(got, gg):
    gg[...] = sum(got[i, 64:80, :].astype(F32) for i in range(8))


def sums_kernel(got, qkv, out):
    cols = []
    for m in range(HL):
        total = got[7 - m].astype(F32) + got[3 - m].astype(F32)
        cols.append(jnp.concatenate([total[20 * l : 20 * l + 20, :] for l in range(3)], axis=1))
    for j in range(3):
        qkv[j] = jnp.concatenate([x[:, j * HD : (j + 1) * HD] for x in cols], axis=1)
    out[...] = jnp.concatenate([x[:, 3 * HD : 4 * HD] for x in cols], axis=1)


def gain_kernel(head, t0, t1, t2, t3, gain, out):
    total = (t0[...] + t1[...] + t2[...] + t3[...])[:10, :] / gain[...]
    flat = jnp.concatenate([total[l : l + 1, :] for l in range(10)], axis=1)
    for j in range(4):
        @pl.when(head[0] == j)
        def _():
            out[...] = flat[0, j * W : (j + 1) * W]


def along_z(x, by):
    return lax.ppermute(x, "z", [(i, i ^ by) for i in range(8)]) if by else x


def along_head(x, by):
    return lax.ppermute(x, HEAD, [(i, i ^ by) for i in range(4)]) if by else x


def to_next_group(x):
    pairs = []
    for i in range(64):
        group = i // 8 + (1 if i % 8 < 4 else -1)
        if 0 <= group < 8:
            pairs.append((i, group * 8 + i % 8))
    return lax.ppermute(x, SEQ, pairs)


def body(patches, gain, w_qkv, w_out, image_ids, cotangent):
    head = lax.axis_index(HEAD).astype(jnp.int32).reshape(1)
    zz = lax.axis_index("z").astype(jnp.int32).reshape(1)
    cot = cotangent.T
    gain = gain.reshape(10, T)
    w = w_qkv.transpose(1, 2, 0).reshape(3 * W, D)
    normed, quarter, x_own, scale_own, inv = call(
        norm_kernel,
        "norm",
        [shape((D, T)), shape((2 * W, T)), shape((W, T)), shape((W, T), F32), shape((8, T), F32)],
        [
            pltpu.VMEM((T, D), BF16),
            pltpu.VMEM((10, T), F32),
            pltpu.VMEM((D, T), BF16),
            pltpu.VMEM((D, T), F32),
            pltpu.SemaphoreType.DMA((3,)),
        ],
        [head],
        patches,
        gain,
        cot,
        far=3,
        limit=60,
    )
    cot, normed = lax.optimization_barrier((cot, normed))
    cots = [along_head(cot, k) for k in range(4)]
    quarter = [quarter, along_z(quarter, 1), None, along_z(quarter, 3)]
    ids = image_ids.reshape(1, T)
    proj = call(project_kernel, "project", shape((3 * W, T)), [], [], normed, w, limit=60)
    own = call(
        payload_kernel,
        "payload",
        [shape((R, T))] * 4,
        [pltpu.VMEM((4, R, T), BF16), pltpu.VMEM((D, T), BF16)],
        [head, zz],
        *cots,
        proj,
        w_out,
        ids,
    )
    own, quarter[1], quarter[3] = lax.optimization_barrier((own, quarter[1], quarter[3]))
    local = {k: along_z(own[k % 4], k) for k in (4, 5, 6, 7, 0, 1, 2, 3)}
    first = jnp.concatenate([quarter[0], quarter[1], quarter[3]], axis=0)
    last = along_z(quarter[3], 1)
    near = call(
        near_kernel,
        "near",
        shape((3, R, T)),
        [pltpu.VMEM((4, R, T), BF16)],
        [zz],
        *[local[k] for k in (4, 5, 6, 7)],
    )
    across = along_head(first, 2)
    near, local[2], local[3] = lax.optimization_barrier((near, local[2], local[3]))
    halo = to_next_group(near)
    quarters = [first, along_head(first, 1), across, along_head(across, 1)]
    across = along_head(last, 2)
    quarters += [last, along_head(last, 1), across, along_head(across, 1)]
    n, c = call(
        assemble_kernel, "assemble", [shape((D, 4 * T))] * 2, [], [head], *quarters
    )
    grads = attention(zz, [local[k] for k in range(8)], halo)
    backs = [grads[k] for k in range(4)]
    terms = call(
        weights_kernel,
        "weights",
        shape((8, 416, T)),
        [pltpu.VMEM((W, 4 * T), BF16), pltpu.VMEM((D, W), F32)],
        [zz],
        n,
        c,
        grads,
        w,
    )
    backs, terms = lax.optimization_barrier((backs, terms))
    terms = lax.all_to_all(terms, ("y", "xh"), 0, 0, tiled=True)
    backs = [along_z(b, k) for k, b in enumerate(backs)]
    pieces = call(
        pieces_kernel,
        "pieces",
        shape((4, 2 * W + IDROWS, T)),
        [pltpu.VMEM((4 * W, T), BF16), pltpu.VMEM((4, 2 * W + IDROWS, T), BF16)],
        [zz, head],
        *backs,
        proj,
        w,
        w_out,
    )
    terms, pieces = lax.optimization_barrier((terms, pieces))
    got = [along_head(pieces[k], k) for k in range(4)]
    terms = call(middle_kernel, "middle", shape((8, 80, T)), [pltpu.VMEM((416, T), F32)], [], terms)
    terms = lax.all_to_all(
        terms, "z", 0, 0, tiled=True, axis_index_groups=[list(range(7, -1, -1))]
    )
    attn_out, grad_patches = call(
        rows_kernel,
        "rows",
        [shape((W, T)), shape((W, T))],
        [],
        [],
        *got,
        x_own,
        scale_own,
        inv,
    )
    gg = call(tails_kernel, "tails", shape((16, T), F32), [], [], terms)
    grad_w_qkv, grad_w_out = call(
        sums_kernel,
        "sums",
        [shape((3, 20, W), F32), shape((20, W), F32)],
        [],
        [],
        terms,
    )
    grad_gain = call(
        gain_kernel, "gain", shape((W,), F32), [], [head], *[along_head(gg, k) for k in range(4)], gain
    )
    return (attn_out.T, grad_patches.T, grad_w_qkv.transpose(1, 0, 2), grad_w_out.T, grad_gain)


def solution(mesh):
    fine = Mesh(mesh.devices.reshape(4, 2, 8, 2, 2), SEQ + HEAD)
    in_specs = (
        P(SEQ, None),
        P(),
        P(None, None, HEAD),
        P(HEAD, None),
        P(SEQ),
        P(SEQ, HEAD),
    )
    out_specs = (
        P(SEQ, HEAD),
        P(SEQ, HEAD),
        P(SEQ, None, HEAD),
        P(HEAD, SEQ),
        P(HEAD),
    )
    return jax.shard_map(body, mesh=fine, in_specs=in_specs, out_specs=out_specs, check_vma=False)
```

```python
import jax
import jax.numpy as jnp
from jax import lax
from jax.experimental import pallas as pl
from jax.experimental.pallas import tpu as pltpu
from jax.sharding import Mesh, PartitionSpec as P

D = 1280
HD = 80
T = 128
HL = 4
W = HL * HD
IDROWS = 16
R = 4 * HD + IDROWS
WIN = 10
OWN = 3
SCALE = HD ** (-0.5)
LOG2E = 1.4426950408889634
SEQ = ("y", "xh", "z")
HEAD = ("xl", "c")
F32 = jnp.float32
BF16 = jnp.bfloat16
LANES = (((1,), (1,)), ((), ()))
GROUPS = ((0, 2, 0, 5), (2, 4, 0, 7), (4, 6, 1, 9), (6, 8, 3, 10), (8, 10, 5, 10))


def call(kernel, name, outs, scratch, scalars, *args, far=0, far_outs=0, limit=12):
    single = not isinstance(outs, (list, tuple))
    vmem, hbm = pl.BlockSpec(memory_space=pltpu.VMEM), pl.BlockSpec(memory_space=pltpu.HBM)
    specs = [pl.BlockSpec(memory_space=pltpu.SMEM)] * len(scalars)
    specs += [vmem] * (len(args) - far) + [hbm] * far
    return pl.pallas_call(
        kernel,
        out_shape=outs,
        in_specs=specs,
        out_specs=vmem if single else [vmem] * (len(outs) - far_outs) + [hbm] * far_outs,
        scratch_shapes=scratch,
        compiler_params=pltpu.CompilerParams(vmem_limit_bytes=limit * 1024 * 1024),
        cost_estimate=pl.CostEstimate(flops=1000, bytes_accessed=1000, transcendentals=0),
        name=name,
    )(*scalars, *args)


def fetch(sems, *pairs):
    copies = [pltpu.make_async_copy(src, dst, sems.at[i]) for i, (src, dst) in enumerate(pairs)]
    for copy in copies:
        copy.start()
    return copies


def shape(dims, dtype=BF16):
    return jax.ShapeDtypeStruct(dims, dtype)


def times(index, size):
    return pl.ds(pl.multiple_of(index * size, size), size)


def norm_kernel(head, patches_far, gain_far, cot_far, normed, quarter, x_own, scale_own, inv_out, patches, gain, xt, scale, sems):
    copies = fetch(sems, (patches_far, patches), (gain_far, gain), (cot_far, quarter.at[W:]))
    copies[0].wait()
    copies[1].wait()
    xt[...] = jnp.transpose(patches[...])
    x = xt[...].astype(F32)
    inv = lax.rsqrt(jnp.sum(x * x, axis=0, keepdims=True) * (1.0 / D) + 1e-06)
    for l in range(10):
        rows = slice(l * T, (l + 1) * T)
        g = jnp.transpose(jnp.broadcast_to(gain[l : l + 1, :], (T, T)))
        scale[rows, :] = inv * g
        normed[rows, :] = (xt[rows, :].astype(F32) * inv * g).astype(BF16)
    inv_out[...] = jnp.broadcast_to(inv, (8, T))
    at = times(head[0], W)
    x_own[...] = xt[at, :]
    scale_own[...] = scale[at, :]
    quarter[:W, :] = normed[at, :]
    copies[2].wait()


def project_kernel(normed, w, proj):
    proj[...] = jnp.dot(w[...], normed[...], preferred_element_type=F32).astype(BF16)


def payload_kernel(head, zz, c0, c1, c2, c3, proj, w_out, ids, e0, e1, e2, e3, own, cot):
    for k, piece in enumerate((c0, c1, c2, c3)):
        cot[times(jnp.bitwise_xor(head[0], k), W), :] = piece[...]
    d_ctx = jnp.dot(w_out[...], cot[...], preferred_element_type=F32).astype(BF16)
    id_rows = jnp.broadcast_to((ids[...] + 1).astype(F32), (IDROWS, T)).astype(BF16)
    for m in range(HL):
        rows = [proj[j * W + m * HD : j * W + (m + 1) * HD, :] for j in range(3)]
        rows = rows + [d_ctx[m * HD : (m + 1) * HD, :], id_rows]
        for j, block in enumerate(rows):
            own[m, j * HD : j * HD + block.shape[0], :] = block
    m = lax.rem(zz[0], 4)
    for k, out in enumerate((e0, e1, e2, e3)):
        out[...] = own[jnp.bitwise_xor(m, k)]


def near_kernel(zz, r4, r5, r6, r7, out, far):
    for i, block in enumerate((r4, r5, r6, r7)):
        far[i] = block[...]
    first = jnp.where(zz[0] < 4, 5, 0)
    for i in range(3):
        out[i] = far[jnp.bitwise_xor(zz[0], first + i) - 4]


def attention_kernel(zz, r0, r1, r2, r3, r4, r5, r6, r7, halo, out, grads, win, kn, vn, idk, es, ds, ps, dss, gk, gv):
    u, m = lax.div(zz[0], 4), lax.rem(zz[0], 4)

    for k, block in enumerate((r0, r1, r2, r3, r4, r5, r6, r7)):
        win[jnp.bitwise_xor(zz[0], k) + jnp.where(u == 0, 4, 0)] = block[...]

    @pl.when(u == 0)
    def _():
        win[1:4] = halo[...]

    @pl.when(u == 1)
    def _():
        win[8:11] = halo[...]

    def rows(c, j):
        return win[1 + c, j * HD : (j + 1) * HD, :]

    def side(first, last, j):
        return jnp.concatenate([rows(c, j) for c in range(first, last)], axis=1)

    ids = [win[1 + c, 4 * HD : 4 * HD + 1, :].astype(F32) for c in range(WIN)]
    for c in range(WIN):
        at = slice(c * T, (c + 1) * T)
        idk[at, :] = jnp.transpose(jnp.broadcast_to(ids[c], (2 * T, T)))
        kn[at, :] = jnp.transpose(rows(c, 1))
        vn[at, :] = jnp.transpose(rows(c, 2))
    gk[...] = jnp.zeros(gk.shape, F32)
    gv[...] = jnp.zeros(gv.shape, F32)
    for qa, qb, ka, kb in GROUPS:
        n = (qb - qa) * T
        qt, dt = side(qa, qb, 0), side(qa, qb, 3)
        idq = jnp.concatenate(ids[qa:qb], axis=1)
        esum = jnp.zeros((1, n), F32)
        dsum = jnp.zeros((1, n), F32)
        for c in range(ka, kb):
            kr = slice(c * T, (c + 1) * T)
            s = jnp.dot(kn[kr, :], qt, preferred_element_type=F32)
            dp = jnp.dot(vn[kr, :], dt, preferred_element_type=F32)
            e = jnp.exp2(jnp.where(idk[kr, :] == idq, s * (SCALE * LOG2E), -1e30))
            es[kr, :] = e
            ds[kr, :] = dp
            esum = esum + jnp.sum(e, axis=0, keepdims=True)
            dsum = dsum + jnp.sum(e * dp, axis=0, keepdims=True)
        r = 1.0 / jnp.maximum(esum, 1e-37)
        delta = dsum * r
        qs, qe = max(qa, OWN), min(qb, OWN + 4)
        ks, ke = max(ka, OWN), min(kb, OWN + 4)
        for c in range(ka, kb) if qs < qe else range(ks, ke):
            kr = slice(c * T, (c + 1) * T)
            p = es[kr, :] * r
            ps[kr, :] = p.astype(BF16)
            dss[kr, :] = (p * (ds[kr, :] - delta)).astype(BF16)
        own = slice(ks * T, ke * T)
        to = slice((ks - OWN) * T, (ke - OWN) * T)
        gk[:, to] += lax.dot_general(qt, dss[own, :], LANES, preferred_element_type=F32)
        gv[:, to] += lax.dot_general(dt, ps[own, :], LANES, preferred_element_type=F32)
        if qs < qe:
            cols = slice((qs - qa) * T, (qe - qa) * T)
            kr = slice(ka * T, kb * T)
            gq = jnp.dot(side(ka, kb, 1), dss[kr, cols], preferred_element_type=F32) * SCALE
            ctx = jnp.dot(side(ka, kb, 2), ps[kr, cols], preferred_element_type=F32)
            for i in range(qe - qs):
                lane = slice(i * T, (i + 1) * T)
                grads[qs - OWN + i, :HD, :] = gq[:, lane].astype(BF16)
                grads[qs - OWN + i, 3 * HD :, :] = ctx[:, lane].astype(BF16)
    for i in range(4):
        lane = slice(i * T, (i + 1) * T)
        grads[i, HD : 2 * HD, :] = (gk[:, lane] * SCALE).astype(BF16)
        grads[i, 2 * HD : 3 * HD, :] = gv[:, lane].astype(BF16)
    for k in range(4):
        out[k] = grads[jnp.bitwise_xor(m, k)]


def attention(zz, locals_, halo):
    big = (WIN * T, 2 * T)
    return call(
        attention_kernel,
        "attention",
        shape((4, 4 * HD, T)),
        [
            pltpu.VMEM((4, 4 * HD, T), BF16),
            pltpu.VMEM((WIN + 2, R, T), BF16),
            pltpu.VMEM((WIN * T, HD), BF16),
            pltpu.VMEM((WIN * T, HD), BF16),
            pltpu.VMEM(big, F32),
            pltpu.VMEM(big, F32),
            pltpu.VMEM(big, F32),
            pltpu.VMEM(big, BF16),
            pltpu.VMEM(big, BF16),
            pltpu.VMEM((HD, 4 * T), F32),
            pltpu.VMEM((HD, 4 * T), F32),
        ],
        [zz],
        *locals_,
        halo,
    )


def pieces_kernel(zz, head, b0, b1, b2, b3, proj, w, w_out, out, grads, parts):
    m = lax.rem(zz[0], 4)
    for k, piece in enumerate((b0, b1, b2, b3)):
        other = jnp.bitwise_xor(m, k)
        for j in range(4):
            grads[times(j * HL + other, HD), :] = piece[j * HD : (j + 1) * HD, :]
    total = jnp.sum(grads[: 3 * W, :].astype(F32) * proj[...].astype(F32), axis=0, keepdims=True)
    hi = total.astype(BF16).astype(F32)
    row = lax.broadcasted_iota(jnp.int32, (IDROWS, T), 0)
    tail = jnp.where(row == 0, hi, jnp.where(row == 1, total - hi, 0.0)).astype(BF16)
    g = jnp.transpose(grads[...])
    d_part = jnp.dot(g[:, : 3 * W], w[...], preferred_element_type=F32)
    out_part = jnp.dot(g[:, 3 * W :], w_out[...], preferred_element_type=F32)
    out_part = jnp.transpose(out_part.astype(BF16))
    d_part = jnp.transpose(d_part.astype(BF16))
    for j in range(4):
        parts[j, :W, :] = out_part[j * W : (j + 1) * W, :]
        parts[j, W : 2 * W, :] = d_part[j * W : (j + 1) * W, :]
        parts[j, 2 * W :, :] = tail
    for k in range(4):
        out[k] = parts[jnp.bitwise_xor(head[0], k)]


def rows_kernel(g0, g1, g2, g3, x_own, scale_own, inv, attn_out, grad_patches):
    total = g0[...].astype(F32) + g1[...].astype(F32) + g2[...].astype(F32) + g3[...].astype(F32)
    attn_out[...] = total[:W, :].astype(BF16)
    d_own = total[W : 2 * W, :]
    x = x_own[...].astype(F32)
    i = inv[0:1, :]
    row_total = total[2 * W : 2 * W + 1, :] + total[2 * W + 1 : 2 * W + 2, :]
    grad_patches[...] = (scale_own[...] * d_own - x * (i * i * row_total * (1.0 / D))).astype(BF16)


def assemble_kernel(head, *refs):
    n, c = refs[8:]
    for j in range(4):
        at = times(jnp.bitwise_xor(head[0], j), W)
        for k, (part, row) in enumerate(((0, 0), (0, 1), (4, 0), (0, 2))):
            lane = slice(k * T, (k + 1) * T)
            n[at, lane] = refs[part + j][2 * row * W : (2 * row + 1) * W, :]
            c[at, lane] = refs[part + j][(2 * row + 1) * W : (2 * row + 2) * W, :]


def weights_kernel(zz, n, c, grads, w, out, g, term):
    m = lax.rem(zz[0], 4)
    for k in range(4):
        g[:, k * T : (k + 1) * T] = grads[k]
    left = lax.dot_general(n[...], g[: 3 * HD, :], LANES, preferred_element_type=F32)
    right = lax.dot_general(c[...], g[3 * HD :, :], LANES, preferred_element_type=F32)
    term[...] = jnp.concatenate([left, right], axis=1)
    turned = lax.dot_general(g[: 3 * HD, :], n[...], LANES, preferred_element_type=F32)
    gg = jnp.zeros((1, D), F32)
    for j in range(3):
        product = turned[j * HD : (j + 1) * HD, :] * w[times(j * HL + m, HD), :].astype(F32)
        gg = gg + jnp.sum(product, axis=0, keepdims=True)
    rows = [gg[:, l * T : (l + 1) * T] for l in range(10)]
    rows = rows + [jnp.zeros((6, T), F32)]
    tail = jnp.concatenate(rows, axis=0).astype(BF16)
    for d in range(8):
        out[d, :160, :] = term[160 * d : 160 * d + 160, :T].astype(BF16)
        out[d, 160:320, :] = term[160 * d : 160 * d + 160, T : 2 * T].astype(BF16)
        halves = [term[160 * d + 80 * i : 160 * d + 80 * i + 80, 2 * T :] for i in range(2)]
        out[d, 320:400, :] = jnp.concatenate(halves, axis=1).astype(BF16)
        out[d, 400:, :] = tail


def middle_kernel(got, out, total):
    total[...] = sum(got[i].astype(F32) for i in range(8))
    zero = jnp.zeros((4, T), F32)
    for z in range(8):
        third = total[320 + 20 * (z % 4) : 340 + 20 * (z % 4), :]
        if z >= 4:
            third = pltpu.roll(third, 64, 1)
        rows = [total[20 * z : 20 * z + 20, :], total[160 + 20 * z : 180 + 20 * z, :], third]
        out[7 - z] = jnp.concatenate(rows + [zero, total[400:, :]], axis=0).astype(BF16)


def tails_kernel(got, gg):
    gg[...] = sum(got[i, 64:80, :].astype(F32) for i in range(8))


def sums_kernel(got, qkv, out):
    cols = []
    for m in range(HL):
        total = got[7 - m].astype(F32) + got[3 - m].astype(F32)
        cols.append(jnp.concatenate([total[20 * l : 20 * l + 20, :] for l in range(3)], axis=1))
    for j in range(3):
        qkv[j] = jnp.concatenate([x[:, j * HD : (j + 1) * HD] for x in cols], axis=1)
    out[...] = jnp.concatenate([x[:, 3 * HD : 4 * HD] for x in cols], axis=1)


def gain_kernel(head, t0, t1, t2, t3, gain, out):
    total = (t0[...] + t1[...] + t2[...] + t3[...])[:10, :] / gain[...]
    flat = jnp.concatenate([total[l : l + 1, :] for l in range(10)], axis=1)
    for j in range(4):
        @pl.when(head[0] == j)
        def _():
            out[...] = flat[0, j * W : (j + 1) * W]


def along_z(x, by):
    return lax.ppermute(x, "z", [(i, i ^ by) for i in range(8)]) if by else x


def along_head(x, by):
    return lax.ppermute(x, HEAD, [(i, i ^ by) for i in range(4)]) if by else x


def to_next_group(x):
    pairs = []
    for i in range(64):
        group = i // 8 + (1 if i % 8 < 4 else -1)
        if 0 <= group < 8:
            pairs.append((i, group * 8 + i % 8))
    return lax.ppermute(x, SEQ, pairs)


def body(patches, gain, w_qkv, w_out, image_ids, cotangent):
    head = lax.axis_index(HEAD).astype(jnp.int32).reshape(1)
    zz = lax.axis_index("z").astype(jnp.int32).reshape(1)
    cot = cotangent.T
    gain = gain.reshape(10, T)
    w = w_qkv.transpose(1, 2, 0).reshape(3 * W, D)
    normed, quarter, x_own, scale_own, inv = call(
        norm_kernel,
        "norm",
        [shape((D, T)), shape((2 * W, T)), shape((W, T)), shape((W, T), F32), shape((8, T), F32)],
        [
            pltpu.VMEM((T, D), BF16),
            pltpu.VMEM((10, T), F32),
            pltpu.VMEM((D, T), BF16),
            pltpu.VMEM((D, T), F32),
            pltpu.SemaphoreType.DMA((3,)),
        ],
        [head],
        patches,
        gain,
        cot,
        far=3,
        limit=60,
    )
    cot, normed = lax.optimization_barrier((cot, normed))
    cots = [along_head(cot, k) for k in range(4)]
    quarter = [quarter, along_z(quarter, 1), None, along_z(quarter, 3)]
    ids = image_ids.reshape(1, T)
    proj = call(project_kernel, "project", shape((3 * W, T)), [], [], normed, w, limit=60)
    own = call(
        payload_kernel,
        "payload",
        [shape((R, T))] * 4,
        [pltpu.VMEM((4, R, T), BF16), pltpu.VMEM((D, T), BF16)],
        [head, zz],
        *cots,
        proj,
        w_out,
        ids,
    )
    own, quarter[1], quarter[3] = lax.optimization_barrier((own, quarter[1], quarter[3]))
    local = {k: along_z(own[k % 4], k) for k in (4, 5, 6, 7, 0, 1, 2, 3)}
    first = jnp.concatenate([quarter[0], quarter[1], quarter[3]], axis=0)
    last = along_z(quarter[3], 1)
    near = call(
        near_kernel,
        "near",
        shape((3, R, T)),
        [pltpu.VMEM((4, R, T), BF16)],
        [zz],
        *[local[k] for k in (4, 5, 6, 7)],
    )
    across = along_head(first, 2)
    near, local[2], local[3] = lax.optimization_barrier((near, local[2], local[3]))
    halo = to_next_group(near)
    quarters = [first, along_head(first, 1), across, along_head(across, 1)]
    across = along_head(last, 2)
    quarters += [last, along_head(last, 1), across, along_head(across, 1)]
    n, c = call(
        assemble_kernel, "assemble", [shape((D, 4 * T))] * 2, [], [head], *quarters
    )
    grads = attention(zz, [local[k] for k in range(8)], halo)
    backs = [grads[k] for k in range(4)]
    terms = call(
        weights_kernel,
        "weights",
        shape((8, 416, T)),
        [pltpu.VMEM((W, 4 * T), BF16), pltpu.VMEM((D, W), F32)],
        [zz],
        n,
        c,
        grads,
        w,
        limit=44,
    )
    backs, terms = lax.optimization_barrier((backs, terms))
    terms = lax.all_to_all(terms, ("y", "xh"), 0, 0, tiled=True)
    backs = [along_z(b, k) for k, b in enumerate(backs)]
    pieces = call(
        pieces_kernel,
        "pieces",
        shape((4, 2 * W + IDROWS, T)),
        [pltpu.VMEM((4 * W, T), BF16), pltpu.VMEM((4, 2 * W + IDROWS, T), BF16)],
        [zz, head],
        *backs,
        proj,
        w,
        w_out,
    )
    terms, pieces = lax.optimization_barrier((terms, pieces))
    got = [along_head(pieces[k], k) for k in range(4)]
    terms = call(middle_kernel, "middle", shape((8, 80, T)), [pltpu.VMEM((416, T), F32)], [], terms)
    terms = lax.all_to_all(
        terms, "z", 0, 0, tiled=True, axis_index_groups=[list(range(7, -1, -1))]
    )
    attn_out, grad_patches = call(
        rows_kernel,
        "rows",
        [shape((W, T)), shape((W, T))],
        [],
        [],
        *got,
        x_own,
        scale_own,
        inv,
    )
    gg = call(tails_kernel, "tails", shape((16, T), F32), [], [], terms)
    grad_w_qkv, grad_w_out = call(
        sums_kernel,
        "sums",
        [shape((3, 20, W), F32), shape((20, W), F32)],
        [],
        [],
        terms,
    )
    grad_gain = call(
        gain_kernel, "gain", shape((W,), F32), [], [head], *[along_head(gg, k) for k in range(4)], gain
    )
    return (attn_out.T, grad_patches.T, grad_w_qkv.transpose(1, 0, 2), grad_w_out.T, grad_gain)


def solution(mesh):
    fine = Mesh(mesh.devices.reshape(4, 2, 8, 2, 2), SEQ + HEAD)
    in_specs = (
        P(SEQ, None),
        P(),
        P(None, None, HEAD),
        P(HEAD, None),
        P(SEQ),
        P(SEQ, HEAD),
    )
    out_specs = (
        P(SEQ, HEAD),
        P(SEQ, HEAD),
        P(SEQ, None, HEAD),
        P(HEAD, SEQ),
        P(HEAD),
    )
    return jax.shard_map(body, mesh=fine, in_specs=in_specs, out_specs=out_specs, check_vma=False)
```
